32 devices in a mesh: parts: 2 (over y), node: 2 (over core), local: 8 (over z, x).
Axes of the slice: x: 2, y: 2, z: 4, core: 2. Of those that a mesh axis runs over, the one named last changes fastest.
Arguments:
- tokens: bfloat16 [2048, 7168], P(('parts', 'node', 'local')), parts along dimension 0, may hold values from -6 to 6
- experts: int32 [2048, 1], P(('parts', 'node', 'local')), parts along dimension 0, may hold values from 0 to 11; in each aligned block of 64 rows (0 to 63, 64 to 127, ...) at most 6 rows name the same one
- replicas: int32 [2048, 1], P(('parts', 'node', 'local')), parts along dimension 0, may hold values from 0 to 1
- gates: float32 [2048, 1], P(('parts', 'node', 'local')), parts along dimension 0, may hold values from 0.2 to 1
- placement: int32 [12, 2], replicated, may hold values from 0 to 15, as said below
- gate_weight: bfloat16 [16, 7168, 2048], P(('node', 'local')), may hold values from -0.0625 to 0.0625
- up_weight: bfloat16 [16, 7168, 2048], P(('node', 'local')), may hold values from -0.0625 to 0.0625
- down_weight: bfloat16 [16, 2048, 7168], P(('node', 'local')), may hold values from -0.125 to 0.125
Outputs:
- mixed: bfloat16 [2048, 7168], P(('parts', 'node', 'local')), parts along dimension 0
The draws below stay inside these ranges and needn't reach their ends.
There are 2 independent parts, one for each index of `parts`. The reference program is written for one: setup_inputs(seed, part) draws one part's arguments, and reference() takes and returns one part's arrays. A program takes and returns all parts, laid end to end along the dimension named above; an argument that names none is the same for every part. Nothing has to cross between parts.
Inputs may be any that keep to these rules, and one draw needn't show every extreme that they name: `placement`: every copy 0 to 15 appears in the table; column 0 names 12 different copies, and column 1 names, for 4 experts, a further copy of their own, for the others the copy of column 0. `experts`: among the 64 tokens of one block no expert is picked more than 6 times, and some block picks some expert exactly 6 times.
All inputs are finite; a program needn't handle non-finite values.
Results may differ from the reference program's by a relative error of at most 0.0057.
Values may be sent and summed in bfloat16 or wider, within the bound.
No kernel may reach another device: no remote copies, remote signals or barrier semaphores. Data moves between devices by JAX's collectives and lax.ppermute only.
A program may use at most 192 MiB of HBM per device.

```python
import math
import jax
import jax.numpy as jnp
import numpy as np
from jax import lax

D = 7168
FF = 2048
TOP = 1
EXPERTS = 12
SLOTS = 16
REPL = 2
TOK_DEV = 64
CAP = 6
HSPLIT = 1
HID_DEV = 2048
TOKENS = 1024
N_NODE = 2
N_LOCAL = 8


def draw_placement(key, part):
    key = jax.random.fold_in(key, 7)
    first_key, second_key = jax.random.split(key)
    shuffled = jax.random.permutation(first_key, SLOTS).astype(jnp.int32)
    copied = jax.random.permutation(second_key, EXPERTS).astype(jnp.int32)[:SLOTS - EXPERTS]
    first_col = shuffled[:EXPERTS]
    spare_slots = shuffled[EXPERTS:]
    matches = (copied[:, None] == jnp.arange(EXPERTS, dtype=jnp.int32)[None, :]).astype(jnp.int32)
    second_col = first_col + jnp.sum(matches * (spare_slots[:, None] - first_col[None, :]), axis=0)
    return jnp.stack([first_col, second_col], axis=1).astype(jnp.int32)


def plant(drawn, stream_key, least, largest):
    dims = drawn.shape
    index_at = [jax.random.randint(jax.random.fold_in(stream_key, axis), (), 0, dims[axis]) for axis in range(len(dims))]
    drawn = drawn.at[tuple(index_at)].set(least)
    longest = dims.index(max(dims))
    index_at[longest] = (index_at[longest] + 1) % dims[longest]
    return drawn.at[tuple(index_at)].set(largest)


def levels(key, shape, pieces, low, largest):
    loudness, own = 1.0, jax.random.fold_in(key, 6)
    for dim, parts in pieces:
        steps = jnp.exp(jax.random.uniform(jax.random.fold_in(own, dim), (parts,), jnp.float32, low / len(pieces), largest / len(pieces)))
        loudness = loudness * jnp.repeat(steps, shape[dim] // parts).reshape([-1 if axis == dim else 1 for axis in range(len(shape))])
    return loudness


def assign_block(own_key, own, number, rows, amount, top, bound, lean):
    sequence = jax.random.permutation(own_key, amount)
    crowded, ordinary = load_shares(amount, rows * top, bound, lean, True), load_shares(amount, rows * top, bound, lean, False)
    places = jnp.arange(amount)

    def named(sizes, turn):
        used = int((sizes > 0).sum())
        fixed = max(1, used // 4)
        passed = fixed + (places - fixed + turn * (used - fixed)) % max(1, amount - fixed)
        return jnp.zeros((amount,), jnp.int32).at[sequence[jnp.where(places < fixed, places, passed)]].set(jnp.asarray(sizes, jnp.int32))

    sizes = jnp.where(number % 4 == 0, named(crowded, number // 4), named(ordinary, number - number // 4 - 1))
    mixed = jax.random.permutation(jax.random.fold_in(own, 3), amount)
    giver, taker = mixed[0:amount // 2 * 2:2], mixed[1:amount // 2 * 2:2]
    margin = jnp.minimum(sizes[giver] - 1, bound - sizes[taker]) // 2
    margin = jnp.where((giver == sequence[0]) | (taker == sequence[0]) | (sizes[taker] == 0), 0, jnp.maximum(margin, 0))
    passed = jax.random.randint(jax.random.fold_in(own, 4), (amount // 2,), 0, 1 << 20) % (margin + 1)
    sizes = sizes.at[giver].add(-passed).at[taker].add(passed)
    items = jnp.searchsorted(jnp.cumsum(sizes), jnp.arange(rows * top), side="right").astype(jnp.int32)
    table = items.reshape(top, rows).T
    table = table[jax.random.permutation(jax.random.fold_in(own, 1), rows)]
    turn = jax.random.randint(jax.random.fold_in(own, 2), (rows, 1), 0, top)
    return jnp.take_along_axis(table, (jnp.arange(top)[None, :] + turn) % top, axis=1)


def load_shares(number_of, total, bound, lean, full):
    portions = [(1 << 20) // math.isqrt(standing ** lean) + 1 for standing in range(1, number_of + 1)]
    largest = bound if full else min(bound, max(-(-total // number_of), total * portions[0] // sum(portions)))
    least = 1 if total - largest >= number_of - 1 else 0
    holding, spare = [largest] + [least] * (number_of - 1), total - largest - least * (number_of - 1)
    while spare > 0:
        free = [i for i in range(1, number_of) if holding[i] < largest] or [i for i in range(1, number_of) if holding[i] < bound]
        pool, remaining = sum([portions[i] for i in free]), spare
        for i in free:
            addition = min(bound - holding[i], max(1, remaining * portions[i] // pool), spare)
            holding[i] = holding[i] + addition
            spare = spare - addition
    return np.array(holding)


def scatter_about(key, extent, deviation, bound, pieces=(), kind=jnp.bfloat16):
    drawn = deviation * jax.random.normal(key, extent, jnp.float32)
    if pieces:
        drawn = drawn * levels(key, extent, pieces, -0.22, 0.18)
    return jnp.clip(drawn, -bound, bound).astype(kind)


def setup_inputs(seed: int = 0, part: int = 0) -> dict:
    key_list = jax.random.split(jax.random.key(seed), 9)
    part_splits = jax.random.split(jax.random.fold_in(key_list[8], part), 9)
    tokens = scatter_about(part_splits[0], (TOKENS, D), 1.0, 6.0, ((0, 16),))
    experts_keys = jax.random.split(jax.random.fold_in(part_splits[1], 1), TOKENS // TOK_DEV)
    experts_turns = jax.random.permutation(jax.random.fold_in(part_splits[1], 3), TOKENS // TOK_DEV)
    experts = jax.vmap(lambda own, number: assign_block(jax.random.fold_in(part_splits[1], 2), own, number, TOK_DEV, EXPERTS, TOP, CAP, 2))(experts_keys, experts_turns).reshape((TOKENS, TOP))
    replicas = plant(jax.random.randint(part_splits[2], (TOKENS, TOP), 0, REPL), jax.random.fold_in(part_splits[2], 1), 0, REPL - 1).astype(jnp.int32)
    gates = jnp.clip(0.2 + 0.8 * jax.random.uniform(part_splits[3], (TOKENS, TOP), jnp.float32) ** levels(part_splits[3], (TOKENS, TOP), ((0, 16),), -0.2, 0.2), 0.2, 1.0)
    placement = draw_placement(jax.random.fold_in(key_list[8], 71), part)
    gate_weight = scatter_about(key_list[5], (SLOTS * HSPLIT, D, HID_DEV), D ** -0.5, 0.0625, ((0, 16),))
    up_weight = scatter_about(key_list[6], (SLOTS * HSPLIT, D, HID_DEV), D ** -0.5, 0.0625, ((0, 16),))
    down_weight = scatter_about(key_list[7], (SLOTS * HSPLIT, HID_DEV, D), FF ** -0.5, 0.125, ((0, 16),))
    return dict(tokens=tokens, experts=experts, replicas=replicas, gates=gates, placement=placement, gate_weight=gate_weight, up_weight=up_weight, down_weight=down_weight)


def route_tables(experts, replicas, gates, placement):
    expert_hit = experts[:, :, None] == jnp.arange(EXPERTS, dtype=jnp.int32)[None, None, :]
    replica_hit = replicas[:, :, None] == jnp.arange(REPL, dtype=jnp.int32)[None, None, :]
    joined = expert_hit[:, :, :, None] & replica_hit[:, :, None, :]
    slot_ids = jnp.sum(jnp.where(joined, placement[None, None, :, :], 0), axis=(2, 3)).astype(jnp.int32)
    flat_slots = slot_ids.reshape(-1)
    slot_hit = (flat_slots[:, None] == jnp.arange(SLOTS, dtype=jnp.int32)[None, :]).astype(jnp.int32)
    before = jnp.cumsum(slot_hit, axis=0).astype(jnp.int32) - slot_hit
    rank = jnp.sum(slot_hit * before, axis=1).astype(jnp.int32)
    position = (flat_slots * CAP + rank).astype(jnp.int32).reshape(slot_ids.shape)
    grid = position[:, :, None] == jnp.arange(SLOTS * CAP, dtype=jnp.int32)[None, None, :]
    scatter = jnp.any(grid, axis=1).T
    zero_gate = jnp.zeros_like(gates)[:, :, None]
    combine = jnp.sum(jnp.where(grid, gates[:, :, None], zero_gate), axis=1)
    return scatter, combine


def reference(tokens, experts, replicas, gates, placement, gate_weight, up_weight, down_weight):
    groups = N_NODE * N_LOCAL
    tok_blocks = tokens.reshape(groups, TOK_DEV, D)
    scatter, combine = jax.vmap(route_tables, in_axes=(0, 0, 0, None))(
        experts.reshape(groups, TOK_DEV, TOP), replicas.reshape(groups, TOK_DEV, TOP),
        gates.reshape(groups, TOK_DEV, TOP), placement)

    def pick_rows(items):
        table, block = items
        return jnp.dot(table.astype(jnp.bfloat16), block, preferred_element_type=jnp.float32).astype(jnp.bfloat16)

    rows = lax.map(pick_rows, (scatter, tok_blocks))
    rows = jnp.moveaxis(rows.reshape(groups, SLOTS, CAP, D), 1, 0).reshape(SLOTS, groups * CAP, D)
    weights = jnp.moveaxis(combine.reshape(groups, TOK_DEV, SLOTS, CAP), 2, 0)
    gate_all = gate_weight.reshape(SLOTS, HSPLIT, D, HID_DEV)
    up_all = up_weight.reshape(SLOTS, HSPLIT, D, HID_DEV)
    down_all = down_weight.reshape(SLOTS, HSPLIT, HID_DEV, D)

    def scan_step(total, items):
        slot_rows, gate_part, up_part, down_part, slot_weights = items
        gate_full = jnp.moveaxis(gate_part, 0, 1).reshape(D, FF)
        up_full = jnp.moveaxis(up_part, 0, 1).reshape(D, FF)
        gate_val = jnp.dot(slot_rows, gate_full, preferred_element_type=jnp.float32)
        up_val = jnp.dot(slot_rows, up_full, preferred_element_type=jnp.float32)
        hidden = (jax.nn.silu(gate_val) * up_val).astype(jnp.bfloat16)
        expert_out = jnp.zeros((groups * CAP, D), jnp.float32)
        for member in range(HSPLIT):
            piece = jnp.dot(hidden[:, member * HID_DEV:(member + 1) * HID_DEV], down_part[member],
                            preferred_element_type=jnp.float32).astype(jnp.bfloat16)
            piece = lax.optimization_barrier(piece)
            expert_out = expert_out + piece.astype(jnp.float32)
        expert_out = expert_out.reshape(groups, CAP, D)
        added = jnp.einsum("gtc,gcd->gtd", slot_weights, expert_out, precision=lax.Precision.HIGHEST)
        return total + added, None

    start_total = jnp.zeros((groups, TOK_DEV, D), jnp.float32)
    total, unused = lax.scan(scan_step, start_total, (rows, gate_all, up_all, down_all, weights))
    return total.reshape(TOKENS, D).astype(jnp.bfloat16)
```

```python
import functools

import jax
import jax.numpy as jnp
import numpy as np
from jax import lax
from jax.experimental import pallas as pl
from jax.experimental.pallas import tpu as pltpu
from jax.sharding import PartitionSpec as P

FF = 2048
CAP = 6
FOLD = 4
STEP = 256
HOPS = (1, 2, 4, 6, 5, 7, 3)
DISPATCH = (1024, 768)
RETURN = (512, 1280)
VMEM_BYTES = 56 * 1024 * 1024


def route_tables(experts, replicas, gates, placement, slot_count, capacity):
    expert_hit = (
        experts[:, :, None] == jnp.arange(placement.shape[0], dtype=jnp.int32)[None, None, :]
    )
    replica_hit = (
        replicas[:, :, None] == jnp.arange(placement.shape[1], dtype=jnp.int32)[None, None, :]
    )
    joined = expert_hit[:, :, :, None] & replica_hit[:, :, None, :]
    slot_ids = jnp.sum(jnp.where(joined, placement[None, None, :, :], 0), axis=(2, 3))
    flat_slots = slot_ids.reshape(-1)
    slot_hit = (flat_slots[:, None] == jnp.arange(slot_count, dtype=jnp.int32)[None, :]).astype(
        jnp.int32
    )
    before = jnp.cumsum(slot_hit, axis=0) - slot_hit
    rank = jnp.sum(slot_hit * before, axis=1)
    position = (flat_slots * capacity + rank).reshape(slot_ids.shape)
    grid = position[:, :, None] == jnp.arange(slot_count * capacity, dtype=jnp.int32)[None, None, :]
    scatter = jnp.any(grid, axis=1).T
    zero_gate = jnp.zeros_like(gates)[:, :, None]
    combine = jnp.sum(jnp.where(grid, gates[:, :, None], zero_gate), axis=1)
    return (scatter, combine)


def per_device_general(
    tokens, experts, replicas, gates, placement, gate_weight, up_weight, down_weight
):
    model_width = tokens.shape[1]
    hidden_dev = gate_weight.shape[2]
    group_size = FF // hidden_dev
    devices_all = lax.axis_size(("node", "local"))
    slot_count = devices_all // group_size
    capacity = CAP
    scatter, combine = route_tables(experts, replicas, gates, placement, slot_count, capacity)
    outgoing = jnp.dot(
        scatter.astype(jnp.bfloat16), tokens, preferred_element_type=jnp.float32
    ).astype(jnp.bfloat16)
    outgoing = outgoing.reshape(slot_count, capacity, model_width)
    sending = jnp.repeat(outgoing, group_size, axis=0)
    arrived = lax.all_to_all(sending, ("node", "local"), split_axis=0, concat_axis=0, tiled=True)
    row_block = arrived.reshape(-1, model_width)
    gate_val = jnp.dot(row_block, gate_weight[0], preferred_element_type=jnp.float32)
    up_val = jnp.dot(row_block, up_weight[0], preferred_element_type=jnp.float32)
    hidden = (jax.nn.silu(gate_val) * up_val).astype(jnp.bfloat16)
    partial_value = (
        jnp.dot(hidden, down_weight[0], preferred_element_type=jnp.float32)
        .astype(jnp.bfloat16)
        .reshape(arrived.shape)
    )
    returned = lax.all_to_all(
        partial_value, ("node", "local"), split_axis=0, concat_axis=0, tiled=True
    )
    summed = jnp.sum(
        returned.reshape(slot_count, group_size, capacity, model_width).astype(jnp.float32), axis=1
    )
    mixed = jnp.dot(
        combine,
        summed.reshape(slot_count * capacity, model_width),
        precision=lax.Precision.HIGHEST,
        preferred_element_type=jnp.float32,
    )
    return mixed.astype(jnp.bfloat16)


def params(**kw):
    return pltpu.CompilerParams(vmem_limit_bytes=VMEM_BYTES, **kw)


def whole(shape):
    return pl.BlockSpec(shape, lambda *_: (0,) * len(shape))


def cost(flops, size):
    return pl.CostEstimate(flops=int(flops), bytes_accessed=int(size), transcendentals=0)


def fold_order(groups):
    g, q, c = np.meshgrid(np.arange(groups), np.arange(FOLD), np.arange(CAP), indexing="ij")
    order = np.zeros(groups * FOLD * CAP, np.int64)
    order[(q * groups * CAP + g * CAP + c).ravel()] = (g * FOLD * CAP + q * CAP + c).ravel()
    return order


def dispatch_kernel(n_local, widths, place_ref, who_ref, pick_ref, own_ref, mate_ref, *outs):
    base_ref, blocks = outs[0], outs[1:]
    tok = own_ref.shape[0]
    both = 2 * tok
    node, local = who_ref[0], who_ref[1]
    pick = pick_ref[...]
    slot = jnp.zeros((1, both), jnp.int32)
    for e in range(place_ref.shape[0]):
        for r in range(place_ref.shape[1]):
            slot = jnp.where(pick == e * place_ref.shape[1] + r, place_ref[e, r], slot)
    slots = 2 * n_local
    hit = lax.broadcasted_iota(jnp.int32, (slots, both), 0) == slot
    early = lax.broadcasted_iota(jnp.int32, (both, both), 0)
    late = lax.broadcasted_iota(jnp.int32, (both, both), 1)
    same_block = (early >= tok) == (late >= tok)
    earlier = ((early < late) & same_block).astype(jnp.bfloat16)
    before = jnp.dot(hit.astype(jnp.bfloat16), earlier, preferred_element_type=jnp.float32)
    rank = jnp.sum(jnp.where(hit, before, 0.0), axis=0, keepdims=True).astype(jnp.int32)
    place_of = slot - node * n_local
    here = (place_of >= 0) & (place_of < n_local)
    hop = place_of ^ local
    second = (lax.broadcasted_iota(jnp.int32, (1, both), 1) >= tok).astype(jnp.int32)
    base = jnp.where(here, (hop * 2 + second) * (FOLD * CAP) + rank, -FOLD * CAP)
    base_ref[...] = base
    rows = slots * FOLD * CAP
    row = lax.broadcasted_iota(jnp.int32, (rows, both), 0)
    select = jnp.concatenate(
        [(row == base + q * CAP).astype(jnp.bfloat16) for q in range(FOLD)], axis=1
    )
    size = 2 * FOLD * CAP
    start = 0
    for piece, width in enumerate(widths):
        folded = jnp.concatenate(
            [
                ref[:, start + q * width : start + (q + 1) * width]
                for q in range(FOLD)
                for ref in (own_ref, mate_ref)
            ],
            axis=0,
        )
        value = jnp.dot(select, folded, preferred_element_type=jnp.float32).astype(jnp.bfloat16)
        for hop_id in range(n_local):
            blocks[piece * n_local + hop_id][...] = value[hop_id * size : (hop_id + 1) * size]
        start += FOLD * width


def dispatch(place, who, pick, own, mate, n_local):
    tok, model = own.shape
    size = 2 * FOLD * CAP
    out_shape = [jax.ShapeDtypeStruct((1, 2 * tok), jnp.int32)] + [
        jax.ShapeDtypeStruct((size, width), jnp.bfloat16)
        for width in DISPATCH
        for _ in range(n_local)
    ]
    smem = pl.BlockSpec(memory_space=pltpu.SMEM)
    vmem = pl.BlockSpec(memory_space=pltpu.VMEM)
    outs = pl.pallas_call(
        functools.partial(dispatch_kernel, n_local, DISPATCH),
        out_shape=out_shape,
        in_specs=[smem, smem, vmem, vmem, vmem],
        out_specs=[vmem] * len(out_shape),
        compiler_params=params(),
        cost_estimate=cost(2e9, 6e6),
        name="dispatch",
    )(place, who, pick, own, mate)
    pieces = [
        outs[1 + i * n_local : 1 + (i + 1) * n_local] for i in range(len(DISPATCH))
    ]
    return outs[0], pieces


def unfold(blocks, order_ref, x_ref, rows, width):
    folded = jnp.concatenate([b[...] for b in blocks], axis=0)
    value = jnp.dot(order_ref[...], folded, preferred_element_type=jnp.float32)
    value = value.astype(jnp.bfloat16)
    tiles = width // STEP
    for q in range(FOLD):
        for j in range(tiles):
            x_ref[q * tiles + j] = value[
                q * rows : (q + 1) * rows, j * STEP : (j + 1) * STEP
            ]


def refold(tiles_ref, order_ref, blocks, width):
    tiles = width // STEP
    value = jnp.concatenate(
        [
            jnp.concatenate([tiles_ref[q * tiles + j] for j in range(tiles)], axis=1)
            for q in range(FOLD)
        ],
        axis=0,
    )
    folded = jnp.dot(order_ref[...], value, preferred_element_type=jnp.float32)
    folded = folded.astype(jnp.bfloat16)
    size = 2 * FOLD * CAP
    for i, block in enumerate(blocks):
        block[...] = folded[i * size : (i + 1) * size]


def first_kernel(n_local, width, order_ref, *refs):
    blocks = refs[:n_local]
    wg_ref, wu_ref, accg_ref, accu_ref, x_ref = refs[n_local:]
    i = pl.program_id(0)
    rows = 2 * n_local * CAP

    @pl.when(i == 0)
    def _():
        unfold(blocks, order_ref, x_ref, rows, width)
        accg_ref[...] = jnp.zeros_like(accg_ref)
        accu_ref[...] = jnp.zeros_like(accu_ref)

    x = x_ref[i]
    accg_ref[...] += jnp.dot(x, wg_ref[0], preferred_element_type=jnp.float32)
    accu_ref[...] += jnp.dot(x, wu_ref[0], preferred_element_type=jnp.float32)


def first_part(order, blocks, gate_weight, up_weight, start, width):
    n_local = len(blocks)
    rows = 2 * n_local * CAP
    hidden = gate_weight.shape[2]
    steps = FOLD * width // STEP
    weight = pl.BlockSpec((1, STEP, hidden), lambda i: (0, start // STEP + i, 0))
    acc = jax.ShapeDtypeStruct((rows, hidden), jnp.float32)
    return pl.pallas_call(
        functools.partial(first_kernel, n_local, width),
        grid=(steps,),
        out_shape=[acc, acc],
        in_specs=[whole(order.shape)] + [whole(b.shape) for b in blocks] + [weight, weight],
        out_specs=[whole(acc.shape)] * 2,
        scratch_shapes=[pltpu.VMEM((steps, rows, STEP), jnp.bfloat16)],
        compiler_params=params(),
        cost_estimate=cost(
            4 * rows * FOLD * width * hidden, 4 * FOLD * width * hidden
        ),
        name="first_part",
    )(order, *blocks, gate_weight, up_weight)


def middle_kernel(n_local, width, width_out, order_ref, back_ref, *refs):
    blocks = refs[:n_local]
    ing_ref, inu_ref, wg_ref, wu_ref, wd_ref = refs[n_local : n_local + 5]
    hidden_ref = refs[n_local + 5]
    outs = refs[n_local + 6 : 2 * n_local + 6]
    x_ref, accg_ref, accu_ref, o_ref = refs[2 * n_local + 6 :]
    i = pl.program_id(0)
    rows = 2 * n_local * CAP
    steps = FOLD * width // STEP
    steps_out = FOLD * width_out // STEP

    @pl.when(i == 0)
    def _():
        unfold(blocks, order_ref, x_ref, rows, width)
        accg_ref[...] = ing_ref[...]
        accu_ref[...] = inu_ref[...]

    @pl.when(i < steps)
    def _():
        x = x_ref[i]
        accg_ref[...] += jnp.dot(x, wg_ref[0], preferred_element_type=jnp.float32)
        accu_ref[...] += jnp.dot(x, wu_ref[0], preferred_element_type=jnp.float32)

    @pl.when(i == steps - 1)
    def _():
        gate_val = accg_ref[...]
        hidden_ref[...] = (gate_val / (1.0 + jnp.exp(-gate_val)) * accu_ref[...]).astype(
            jnp.bfloat16
        )

    @pl.when(i >= steps)
    def _():
        o_ref[i - steps] = jnp.dot(
            hidden_ref[...], wd_ref[0], preferred_element_type=jnp.float32
        ).astype(jnp.bfloat16)

    @pl.when(i == steps + steps_out - 1)
    def _():
        refold(o_ref, back_ref, outs, width_out)


def middle_part(
    order, back, blocks, accs, gate_weight, up_weight, down_weight, start, width, width_out
):
    n_local = len(blocks)
    rows = 2 * n_local * CAP
    hidden = gate_weight.shape[2]
    steps = FOLD * width // STEP
    steps_out = FOLD * width_out // STEP
    weight = pl.BlockSpec(
        (1, STEP, hidden), lambda i: (0, start // STEP + jnp.minimum(i, steps - 1), 0)
    )
    down = pl.BlockSpec((1, hidden, STEP), lambda i: (0, 0, jnp.maximum(i - steps, 0)))
    size = 2 * FOLD * CAP
    out_shape = [jax.ShapeDtypeStruct((rows, hidden), jnp.bfloat16)] + [
        jax.ShapeDtypeStruct((size, width_out), jnp.bfloat16) for _ in range(n_local)
    ]
    outs = pl.pallas_call(
        functools.partial(middle_kernel, n_local, width, width_out),
        grid=(steps + steps_out,),
        out_shape=out_shape,
        in_specs=[whole(order.shape), whole(back.shape)]
        + [whole(b.shape) for b in blocks]
        + [whole(a.shape) for a in accs]
        + [weight, weight, down],
        out_specs=[whole(o.shape) for o in out_shape],
        scratch_shapes=[
            pltpu.VMEM((steps, rows, STEP), jnp.bfloat16),
            pltpu.VMEM((rows, hidden), jnp.float32),
            pltpu.VMEM((rows, hidden), jnp.float32),
            pltpu.VMEM((steps_out, rows, STEP), jnp.bfloat16),
        ],
        compiler_params=params(),
        cost_estimate=cost(
            2 * rows * FOLD * (2 * width + width_out) * hidden,
            2 * FOLD * (2 * width + width_out) * hidden,
        ),
        name="middle_part",
    )(order, back, *blocks, *accs, gate_weight, up_weight, down_weight)
    return outs[0], outs[1:]


def last_kernel(n_local, width, back_ref, hidden_ref, wd_ref, *refs):
    outs, o_ref = refs[:n_local], refs[n_local]
    i = pl.program_id(0)
    o_ref[i] = jnp.dot(hidden_ref[...], wd_ref[0], preferred_element_type=jnp.float32).astype(
        jnp.bfloat16
    )

    @pl.when(i == pl.num_programs(0) - 1)
    def _():
        refold(o_ref, back_ref, outs, width)


def last_part(back, hidden, down_weight, start, width, n_local):
    rows, inner = hidden.shape
    steps = FOLD * width // STEP
    size = 2 * FOLD * CAP
    out_shape = [jax.ShapeDtypeStruct((size, width), jnp.bfloat16) for _ in range(n_local)]
    return pl.pallas_call(
        functools.partial(last_kernel, n_local, width),
        grid=(steps,),
        out_shape=out_shape,
        in_specs=[
            whole(back.shape),
            whole(hidden.shape),
            pl.BlockSpec((1, inner, STEP), lambda i: (0, 0, start // STEP + i)),
        ],
        out_specs=[whole(o.shape) for o in out_shape],
        scratch_shapes=[pltpu.VMEM((steps, rows, STEP), jnp.bfloat16)],
        compiler_params=params(),
        cost_estimate=cost(
            2 * rows * FOLD * width * inner, 2 * FOLD * width * inner
        ),
        name="last_part",
    )(back, hidden, down_weight)


def column(row):
    n = row.shape[1]
    eye = lax.broadcasted_iota(jnp.int32, (n, n), 0) == lax.broadcasted_iota(jnp.int32, (n, n), 1)
    return jnp.sum(jnp.where(eye, row, jnp.zeros_like(row)), axis=1, keepdims=True)


def pick_kernel(n_local, base_ref, *refs):
    blocks = refs[:n_local]
    own_ref, mate_ref = refs[n_local:]
    tok = own_ref.shape[0]
    width = blocks[0].shape[1]
    base = column(base_ref[...])
    folded = jnp.concatenate([b[...] for b in blocks], axis=0)
    lane = lax.broadcasted_iota(jnp.int32, (base.shape[0], folded.shape[0]), 1)
    for q in range(FOLD):
        select = (lane == base + q * CAP).astype(jnp.bfloat16)
        value = jnp.dot(select, folded, preferred_element_type=jnp.float32).astype(jnp.bfloat16)
        own_ref[:, q * width : (q + 1) * width] = value[:tok]
        mate_ref[:, q * width : (q + 1) * width] = value[tok:]


def pick_rows(base, blocks):
    n_local = len(blocks)
    tok = base.shape[1] // 2
    width = blocks[0].shape[1]
    vmem = pl.BlockSpec(memory_space=pltpu.VMEM)
    half = jax.ShapeDtypeStruct((tok, FOLD * width), jnp.bfloat16)
    return pl.pallas_call(
        functools.partial(pick_kernel, n_local),
        out_shape=[half, half],
        in_specs=[vmem] * (1 + n_local),
        out_specs=[vmem] * 2,
        compiler_params=params(),
        cost_estimate=cost(8 * tok * width * 384 * 2, 6 * tok * FOLD * width),
        name="pick_rows",
    )(base, *blocks)


def mix_kernel(count, gates_ref, *refs):
    own, other, out_ref = refs[:count], refs[count : 2 * count], refs[2 * count]
    gate = column(gates_ref[...])
    start = 0
    for a, b in zip(own, other):
        width = a.shape[1]
        total = a[...].astype(jnp.float32) + b[...].astype(jnp.float32)
        out_ref[:, start : start + width] = (gate * total).astype(jnp.bfloat16)
        start += width


def mix(gates, own, other):
    tok = own[0].shape[0]
    model = sum(a.shape[1] for a in own)
    vmem = pl.BlockSpec(memory_space=pltpu.VMEM)
    return pl.pallas_call(
        functools.partial(mix_kernel, len(own)),
        out_shape=jax.ShapeDtypeStruct((tok, model), jnp.bfloat16),
        in_specs=[vmem] * (1 + 2 * len(own)),
        out_specs=vmem,
        compiler_params=params(),
        cost_estimate=cost(3 * tok * model, 6 * tok * model),
        name="mix",
    )(gates, *own, *other)


def swap_hops(blocks):
    n_local = len(blocks)
    out = list(blocks)
    for hop in HOPS:
        if hop < n_local:
            out[hop] = lax.ppermute(
                blocks[hop], "local", [(i, i ^ hop) for i in range(n_local)]
            )
    return out


def swap_mate(value):
    return lax.ppermute(value, "node", [(0, 1), (1, 0)])


def per_device_folded(
    tokens, experts, replicas, gates, placement, gate_weight, up_weight, down_weight
):
    tok = tokens.shape[0]
    n_local = lax.axis_size("local")
    pick = (experts * placement.shape[1] + replicas).reshape(1, tok)
    mate_tokens = swap_mate(tokens)
    picks = jnp.concatenate([pick, swap_mate(pick)], axis=1)
    who = jnp.stack([lax.axis_index("node"), lax.axis_index("local")]).astype(jnp.int32)
    order = fold_order(2 * n_local)
    size = order.shape[0]
    forward = np.zeros((size, size), np.float32)
    forward[np.arange(size), order] = 1.0
    unfold_order = jnp.asarray(forward, jnp.bfloat16)
    refold_order = jnp.asarray(forward.T, jnp.bfloat16)

    base, pieces = dispatch(placement, who, picks, tokens, mate_tokens, n_local)
    arrived = [swap_hops(piece) for piece in pieces]
    accs = first_part(unfold_order, arrived[0], gate_weight, up_weight, 0, DISPATCH[0])
    hidden, back_first = middle_part(
        unfold_order,
        refold_order,
        arrived[1],
        accs,
        gate_weight,
        up_weight,
        down_weight,
        FOLD * DISPATCH[0],
        DISPATCH[1],
        RETURN[0],
    )
    returned = [swap_hops(back_first)]
    back_second = last_part(
        refold_order, hidden, down_weight, FOLD * RETURN[0], RETURN[1], n_local
    )
    returned.append(swap_hops(back_second))
    picked = [pick_rows(base, blocks) for blocks in returned]
    other = [swap_mate(pair[1]) for pair in picked]
    return mix(gates.reshape(1, tok), [pair[0] for pair in picked], other)


def solution(mesh):
    in_specs = (
        P(("parts", "node", "local"), None),
        P(("parts", "node", "local"), None),
        P(("parts", "node", "local"), None),
        P(("parts", "node", "local"), None),
        P(),
        P(("node", "local"), None, None),
        P(("node", "local"), None, None),
        P(("node", "local"), None, None),
    )
    out_specs = P(("parts", "node", "local"), None)

    def per_device(*args):
        folded = (
            mesh.shape["node"] == 2
            and mesh.shape["local"] == 8
            and args[5].shape[2] == FF
            and args[0].shape[1] == FOLD * sum(DISPATCH)
        )
        return (per_device_folded if folded else per_device_general)(*args)

    return jax.shard_map(
        per_device, mesh=mesh, in_specs=in_specs, out_specs=out_specs, check_vma=False
    )
```

```python
import functools

import jax
import jax.numpy as jnp
import numpy as np
from jax import lax
from jax.experimental import pallas as pl
from jax.experimental.pallas import tpu as pltpu
from jax.sharding import PartitionSpec as P

FF = 2048
CAP = 6
FOLD = 4
STEP = 512
DEPTH = 8
DISPATCH = (1280, 512)
RETURN = (256, 1536)
VMEM_BYTES = 56 * 1024 * 1024


def route_tables(experts, replicas, gates, placement, slot_count, capacity):
    expert_hit = (
        experts[:, :, None] == jnp.arange(placement.shape[0], dtype=jnp.int32)[None, None, :]
    )
    replica_hit = (
        replicas[:, :, None] == jnp.arange(placement.shape[1], dtype=jnp.int32)[None, None, :]
    )
    joined = expert_hit[:, :, :, None] & replica_hit[:, :, None, :]
    slot_ids = jnp.sum(jnp.where(joined, placement[None, None, :, :], 0), axis=(2, 3))
    flat_slots = slot_ids.reshape(-1)
    slot_hit = (flat_slots[:, None] == jnp.arange(slot_count, dtype=jnp.int32)[None, :]).astype(
        jnp.int32
    )
    before = jnp.cumsum(slot_hit, axis=0) - slot_hit
    rank = jnp.sum(slot_hit * before, axis=1)
    position = (flat_slots * capacity + rank).reshape(slot_ids.shape)
    grid = position[:, :, None] == jnp.arange(slot_count * capacity, dtype=jnp.int32)[None, None, :]
    scatter = jnp.any(grid, axis=1).T
    zero_gate = jnp.zeros_like(gates)[:, :, None]
    combine = jnp.sum(jnp.where(grid, gates[:, :, None], zero_gate), axis=1)
    return (scatter, combine)


def per_device_general(
    tokens, experts, replicas, gates, placement, gate_weight, up_weight, down_weight
):
    model_width = tokens.shape[1]
    hidden_dev = gate_weight.shape[2]
    group_size = FF // hidden_dev
    devices_all = lax.axis_size(("node", "local"))
    slot_count = devices_all // group_size
    capacity = CAP
    scatter, combine = route_tables(experts, replicas, gates, placement, slot_count, capacity)
    outgoing = jnp.dot(
        scatter.astype(jnp.bfloat16), tokens, preferred_element_type=jnp.float32
    ).astype(jnp.bfloat16)
    outgoing = outgoing.reshape(slot_count, capacity, model_width)
    sending = jnp.repeat(outgoing, group_size, axis=0)
    arrived = lax.all_to_all(sending, ("node", "local"), split_axis=0, concat_axis=0, tiled=True)
    row_block = arrived.reshape(-1, model_width)
    gate_val = jnp.dot(row_block, gate_weight[0], preferred_element_type=jnp.float32)
    up_val = jnp.dot(row_block, up_weight[0], preferred_element_type=jnp.float32)
    hidden = (jax.nn.silu(gate_val) * up_val).astype(jnp.bfloat16)
    partial_value = (
        jnp.dot(hidden, down_weight[0], preferred_element_type=jnp.float32)
        .astype(jnp.bfloat16)
        .reshape(arrived.shape)
    )
    returned = lax.all_to_all(
        partial_value, ("node", "local"), split_axis=0, concat_axis=0, tiled=True
    )
    summed = jnp.sum(
        returned.reshape(slot_count, group_size, capacity, model_width).astype(jnp.float32), axis=1
    )
    mixed = jnp.dot(
        combine,
        summed.reshape(slot_count * capacity, model_width),
        precision=lax.Precision.HIGHEST,
        preferred_element_type=jnp.float32,
    )
    return mixed.astype(jnp.bfloat16)


def params(**kw):
    return pltpu.CompilerParams(vmem_limit_bytes=VMEM_BYTES, **kw)


VMEM = pl.BlockSpec(memory_space=pltpu.VMEM)
SMEM = pl.BlockSpec(memory_space=pltpu.SMEM)
HBM = pl.BlockSpec(memory_space=pl.ANY)


def cost(flops, size):
    return pl.CostEstimate(flops=int(flops), bytes_accessed=int(size), transcendentals=0)


def fold_matrix(groups):
    g, q, c = np.meshgrid(np.arange(groups), np.arange(FOLD), np.arange(CAP), indexing="ij")
    size = groups * FOLD * CAP
    matrix = np.zeros((size, size), np.float32)
    matrix[
        (q * groups * CAP + g * CAP + c).ravel(), (g * FOLD * CAP + q * CAP + c).ravel()
    ] = 1.0
    return matrix


def dispatch_kernel(widths, place_ref, experts_ref, replicas_ref, tokens_ref, base_ref, *pieces):
    tok = tokens_ref.shape[0]
    rows = pieces[0].shape[0]
    slots = rows // (FOLD * CAP)
    experts, replicas = experts_ref[...], replicas_ref[...]
    slot = jnp.zeros((1, tok), jnp.int32)
    for r in range(place_ref.shape[0]):
        for e in range(place_ref.shape[1]):
            slot = jnp.where((experts == e) & (replicas == r), place_ref[r, e], slot)
    hit = lax.broadcasted_iota(jnp.int32, (slots, tok), 0) == slot
    earlier = lax.broadcasted_iota(jnp.int32, (tok, tok), 0) < lax.broadcasted_iota(
        jnp.int32, (tok, tok), 1
    )
    before = jnp.dot(
        hit.astype(jnp.bfloat16), earlier.astype(jnp.bfloat16), preferred_element_type=jnp.float32
    )
    rank = jnp.sum(jnp.where(hit, before, 0.0), axis=0, keepdims=True).astype(jnp.int32)
    base = slot * (FOLD * CAP) + rank
    base_ref[...] = base
    row = lax.broadcasted_iota(jnp.int32, (rows, tok), 0)
    select = jnp.concatenate(
        [(row == base + q * CAP).astype(jnp.bfloat16) for q in range(FOLD)], axis=1
    )
    start = 0
    for piece, width in zip(pieces, widths):
        folded = jnp.concatenate(
            [tokens_ref[:, start + q * width : start + (q + 1) * width] for q in range(FOLD)],
            axis=0,
        )
        piece[...] = jnp.dot(select, folded, preferred_element_type=jnp.float32).astype(
            jnp.bfloat16
        )
        start += FOLD * width


def dispatch(placement, experts, replicas, tokens, slots):
    tok, model = tokens.shape
    rows = slots * FOLD * CAP
    out_shape = [jax.ShapeDtypeStruct((1, tok), jnp.int32)] + [
        jax.ShapeDtypeStruct((rows, width), jnp.bfloat16) for width in DISPATCH
    ]
    return pl.pallas_call(
        functools.partial(dispatch_kernel, DISPATCH),
        out_shape=out_shape,
        in_specs=[SMEM, VMEM, VMEM, VMEM],
        out_specs=[VMEM] * len(out_shape),
        compiler_params=params(),
        cost_estimate=cost(2 * rows * tok * model, 5 * tok * model),
        name="dispatch",
    )(placement.T, experts.reshape(1, tok), replicas.reshape(1, tok), tokens)


class Stream:
    def __init__(self, buffer, sems, tiles):
        self.depth = buffer.shape[0]
        self.buffer = buffer
        self.copies = []
        for n, tile in enumerate(tiles):
            slot = n % self.depth
            self.copies.append(
                pltpu.make_async_copy(tile, buffer.at[slot], sems.at[slot])
            )
        self.begun = 0

    def ahead(self, upto):
        while self.begun < min(upto, len(self.copies)):
            self.copies[self.begun].start()
            self.begun += 1

    def take(self, n):
        self.ahead(n + 1)
        self.copies[n].wait()
        return self.buffer[n % self.depth]

    def free(self, n):
        self.ahead(n + 1 + self.depth)


def unfold(block_ref, order_ref, x_ref):
    rows, width = x_ref.shape[0], block_ref.shape[1]
    value = jnp.dot(order_ref[...], block_ref[...], preferred_element_type=jnp.float32)
    value = value.astype(jnp.bfloat16)
    for q in range(FOLD):
        x_ref[:, q * width : (q + 1) * width] = value[q * rows : (q + 1) * rows]


def refold(o_ref, order_ref, block_ref):
    width = block_ref.shape[1]
    value = jnp.concatenate(
        [o_ref[:, q * width : (q + 1) * width] for q in range(FOLD)], axis=0
    )
    block_ref[...] = jnp.dot(
        order_ref[...], value, preferred_element_type=jnp.float32
    ).astype(jnp.bfloat16)


def project(x_ref, tiles, accg_ref, accu_ref, fresh):
    for n in range(x_ref.shape[1] // STEP):
        x = x_ref[:, n * STEP : (n + 1) * STEP]
        for m, acc in enumerate((accg_ref, accu_ref)):
            value = jnp.dot(x, tiles.take(2 * n + m), preferred_element_type=jnp.float32)
            acc[...] = value if fresh and n == 0 else acc[...] + value
            tiles.free(2 * n + m)


def in_tiles(wg_ref, wu_ref, start, count):
    return [
        w.at[0, pl.ds(start + n * STEP, STEP)] for n in range(count) for w in (wg_ref, wu_ref)
    ]


def out_tiles(wd_ref, start, count):
    return [wd_ref.at[0, :, pl.ds(start + n * STEP, STEP)] for n in range(count)]


def first_kernel(start, order_ref, block_ref, wg_ref, wu_ref, accg_ref, accu_ref, x_ref, w_ref, sem):
    tiles = Stream(w_ref, sem, in_tiles(wg_ref, wu_ref, start, x_ref.shape[1] // STEP))
    tiles.ahead(tiles.depth)
    unfold(block_ref, order_ref, x_ref)
    project(x_ref, tiles, accg_ref, accu_ref, True)


def first_part(order, block, gate_weight, up_weight, start):
    rows = block.shape[0] // FOLD
    model, hidden = FOLD * block.shape[1], gate_weight.shape[2]
    acc = jax.ShapeDtypeStruct((rows, hidden), jnp.float32)
    return pl.pallas_call(
        functools.partial(first_kernel, start),
        out_shape=[acc, acc],
        in_specs=[VMEM, VMEM, HBM, HBM],
        out_specs=[VMEM, VMEM],
        scratch_shapes=[
            pltpu.VMEM((rows, model), jnp.bfloat16),
            pltpu.VMEM((DEPTH, STEP, hidden), jnp.bfloat16),
            pltpu.SemaphoreType.DMA((DEPTH,)),
        ],
        compiler_params=params(),
        cost_estimate=cost(4 * rows * model * hidden, 4 * model * hidden),
        name="first_part",
    )(order, block, gate_weight, up_weight)


def down(hidden_ref, tiles, o_ref):
    for n in range(o_ref.shape[1] // STEP):
        o_ref[:, n * STEP : (n + 1) * STEP] = jnp.dot(
            hidden_ref[...], tiles.take(n), preferred_element_type=jnp.float32
        ).astype(jnp.bfloat16)
        tiles.free(n)


def middle_kernel(
    start,
    order_ref,
    back_ref,
    block_ref,
    ing_ref,
    inu_ref,
    wg_ref,
    wu_ref,
    wd_ref,
    hidden_ref,
    out_ref,
    x_ref,
    accg_ref,
    accu_ref,
    o_ref,
    w_ref,
    d_ref,
    sem,
    dsem,
):
    tiles = Stream(w_ref, sem, in_tiles(wg_ref, wu_ref, start, x_ref.shape[1] // STEP))
    outs = Stream(d_ref, dsem, out_tiles(wd_ref, 0, o_ref.shape[1] // STEP))
    tiles.ahead(tiles.depth)
    outs.ahead(outs.depth)
    unfold(block_ref, order_ref, x_ref)
    accg_ref[...] = ing_ref[...]
    accu_ref[...] = inu_ref[...]
    project(x_ref, tiles, accg_ref, accu_ref, False)
    gate_val = accg_ref[...]
    hidden_ref[...] = (gate_val / (1.0 + jnp.exp(-gate_val)) * accu_ref[...]).astype(jnp.bfloat16)
    down(hidden_ref, outs, o_ref)
    refold(o_ref, back_ref, out_ref)


def middle_part(order, back, block, accs, gate_weight, up_weight, down_weight, start):
    rows = block.shape[0] // FOLD
    model, hidden = FOLD * block.shape[1], gate_weight.shape[2]
    model_out = FOLD * RETURN[0]
    out_depth = min(DEPTH // 2, model_out // STEP)
    return pl.pallas_call(
        functools.partial(middle_kernel, start),
        out_shape=[
            jax.ShapeDtypeStruct((rows, hidden), jnp.bfloat16),
            jax.ShapeDtypeStruct((block.shape[0], RETURN[0]), jnp.bfloat16),
        ],
        in_specs=[VMEM] * 5 + [HBM] * 3,
        out_specs=[VMEM, VMEM],
        scratch_shapes=[
            pltpu.VMEM((rows, model), jnp.bfloat16),
            pltpu.VMEM((rows, hidden), jnp.float32),
            pltpu.VMEM((rows, hidden), jnp.float32),
            pltpu.VMEM((rows, model_out), jnp.bfloat16),
            pltpu.VMEM((DEPTH, STEP, hidden), jnp.bfloat16),
            pltpu.VMEM((out_depth, hidden, STEP), jnp.bfloat16),
            pltpu.SemaphoreType.DMA((DEPTH,)),
            pltpu.SemaphoreType.DMA((out_depth,)),
        ],
        compiler_params=params(),
        cost_estimate=cost(
            2 * rows * (2 * model + model_out) * hidden, 2 * (2 * model + model_out) * hidden
        ),
        name="middle_part",
    )(order, back, block, *accs, gate_weight, up_weight, down_weight)


def last_kernel(start, back_ref, hidden_ref, wd_ref, out_ref, o_ref, d_ref, dsem):
    outs = Stream(d_ref, dsem, out_tiles(wd_ref, start, o_ref.shape[1] // STEP))
    outs.ahead(outs.depth)
    down(hidden_ref, outs, o_ref)
    refold(o_ref, back_ref, out_ref)


def last_part(back, hidden, down_weight, start, width):
    rows, inner = hidden.shape
    model_out = FOLD * width
    return pl.pallas_call(
        functools.partial(last_kernel, start),
        out_shape=jax.ShapeDtypeStruct((FOLD * rows, width), jnp.bfloat16),
        in_specs=[VMEM, VMEM, HBM],
        out_specs=VMEM,
        scratch_shapes=[
            pltpu.VMEM((rows, model_out), jnp.bfloat16),
            pltpu.VMEM((DEPTH, inner, STEP), jnp.bfloat16),
            pltpu.SemaphoreType.DMA((DEPTH,)),
        ],
        compiler_params=params(),
        cost_estimate=cost(2 * rows * model_out * inner, 2 * model_out * inner),
        name="last_part",
    )(back, hidden, down_weight)


def column(row):
    n = row.shape[1]
    eye = lax.broadcasted_iota(jnp.int32, (n, n), 0) == lax.broadcasted_iota(jnp.int32, (n, n), 1)
    return jnp.sum(jnp.where(eye, row, jnp.zeros_like(row)), axis=1, keepdims=True)


def finish_kernel(base_ref, gates_ref, *refs):
    pieces, out_ref = refs[:-1], refs[-1]
    base = column(base_ref[...])
    gate = column(gates_ref[...])
    lane = lax.broadcasted_iota(jnp.int32, (base.shape[0], pieces[0].shape[0]), 1)
    select = [(lane == base + q * CAP).astype(jnp.bfloat16) for q in range(FOLD)]
    start = 0
    for piece in pieces:
        width = piece.shape[1]
        for q in range(FOLD):
            value = jnp.dot(select[q], piece[...], preferred_element_type=jnp.float32)
            out_ref[:, start : start + width] = (gate * value).astype(jnp.bfloat16)
            start += width


def finish(base, gates, pieces):
    tok = base.shape[1]
    model = FOLD * sum(p.shape[1] for p in pieces)
    return pl.pallas_call(
        finish_kernel,
        out_shape=jax.ShapeDtypeStruct((tok, model), jnp.bfloat16),
        in_specs=[VMEM] * (2 + len(pieces)),
        out_specs=VMEM,
        compiler_params=params(),
        cost_estimate=cost(2 * tok * model * 384, 5 * tok * model),
        name="finish",
    )(base, gates.reshape(1, tok), *pieces)


def swap(block, slots):
    rows, width = block.shape
    out = lax.all_to_all(
        block.reshape(slots, rows // slots, width),
        ("node", "local"),
        split_axis=0,
        concat_axis=0,
        tiled=True,
    )
    return out.reshape(rows, width)


def per_device_folded(
    tokens, experts, replicas, gates, placement, gate_weight, up_weight, down_weight
):
    slots = lax.axis_size(("node", "local"))
    matrix = fold_matrix(slots)
    order = jnp.asarray(matrix, jnp.bfloat16)
    back = jnp.asarray(matrix.T, jnp.bfloat16)
    base, *pieces = dispatch(placement, experts, replicas, tokens, slots)
    arrived = [swap(piece, slots) for piece in pieces]
    accs = first_part(order, arrived[0], gate_weight, up_weight, 0)
    hidden, back_first = middle_part(
        order, back, arrived[1], accs, gate_weight, up_weight, down_weight, FOLD * DISPATCH[0]
    )
    returned = [swap(back_first, slots)]
    back_second = last_part(back, hidden, down_weight, FOLD * RETURN[0], RETURN[1])
    returned.append(swap(back_second, slots))
    return finish(base, gates, returned)


def solution(mesh):
    in_specs = (
        P(("parts", "node", "local"), None),
        P(("parts", "node", "local"), None),
        P(("parts", "node", "local"), None),
        P(("parts", "node", "local"), None),
        P(),
        P(("node", "local"), None, None),
        P(("node", "local"), None, None),
        P(("node", "local"), None, None),
    )
    out_specs = P(("parts", "node", "local"), None)

    def per_device(*args):
        folded = (
            mesh.shape["node"] * mesh.shape["local"] == 16
            and args[1].shape[1] == 1
            and args[5].shape[2] == FF
            and args[0].shape[1] == FOLD * sum(DISPATCH)
        )
        return (per_device_folded if folded else per_device_general)(*args)

    return jax.shard_map(
        per_device, mesh=mesh, in_specs=in_specs, out_specs=out_specs, check_vma=False
    )
```

```python
import functools

import jax
import jax.numpy as jnp
import numpy as np
from jax import lax
from jax.experimental import pallas as pl
from jax.experimental.pallas import tpu as pltpu
from jax.sharding import PartitionSpec as P

FF = 2048
CAP = 6
FOLD = 4
STEP = 512
DEPTH = 8
DISPATCH = (1024, 768)
BACK_COLUMNS = 512
VMEM_BYTES = 56 * 1024 * 1024


def route_tables(experts, replicas, gates, placement, slot_count, capacity):
    expert_hit = (
        experts[:, :, None] == jnp.arange(placement.shape[0], dtype=jnp.int32)[None, None, :]
    )
    replica_hit = (
        replicas[:, :, None] == jnp.arange(placement.shape[1], dtype=jnp.int32)[None, None, :]
    )
    joined = expert_hit[:, :, :, None] & replica_hit[:, :, None, :]
    slot_ids = jnp.sum(jnp.where(joined, placement[None, None, :, :], 0), axis=(2, 3))
    flat_slots = slot_ids.reshape(-1)
    slot_hit = (flat_slots[:, None] == jnp.arange(slot_count, dtype=jnp.int32)[None, :]).astype(
        jnp.int32
    )
    before = jnp.cumsum(slot_hit, axis=0) - slot_hit
    rank = jnp.sum(slot_hit * before, axis=1)
    position = (flat_slots * capacity + rank).reshape(slot_ids.shape)
    grid = position[:, :, None] == jnp.arange(slot_count * capacity, dtype=jnp.int32)[None, None, :]
    scatter = jnp.any(grid, axis=1).T
    zero_gate = jnp.zeros_like(gates)[:, :, None]
    combine = jnp.sum(jnp.where(grid, gates[:, :, None], zero_gate), axis=1)
    return (scatter, combine)


def per_device_general(
    tokens, experts, replicas, gates, placement, gate_weight, up_weight, down_weight
):
    model_width = tokens.shape[1]
    hidden_dev = gate_weight.shape[2]
    group_size = FF // hidden_dev
    devices_all = lax.axis_size(("node", "local"))
    slot_count = devices_all // group_size
    capacity = CAP
    scatter, combine = route_tables(experts, replicas, gates, placement, slot_count, capacity)
    outgoing = jnp.dot(
        scatter.astype(jnp.bfloat16), tokens, preferred_element_type=jnp.float32
    ).astype(jnp.bfloat16)
    outgoing = outgoing.reshape(slot_count, capacity, model_width)
    sending = jnp.repeat(outgoing, group_size, axis=0)
    arrived = lax.all_to_all(sending, ("node", "local"), split_axis=0, concat_axis=0, tiled=True)
    row_block = arrived.reshape(-1, model_width)
    gate_val = jnp.dot(row_block, gate_weight[0], preferred_element_type=jnp.float32)
    up_val = jnp.dot(row_block, up_weight[0], preferred_element_type=jnp.float32)
    hidden = (jax.nn.silu(gate_val) * up_val).astype(jnp.bfloat16)
    partial_value = (
        jnp.dot(hidden, down_weight[0], preferred_element_type=jnp.float32)
        .astype(jnp.bfloat16)
        .reshape(arrived.shape)
    )
    returned = lax.all_to_all(
        partial_value, ("node", "local"), split_axis=0, concat_axis=0, tiled=True
    )
    summed = jnp.sum(
        returned.reshape(slot_count, group_size, capacity, model_width).astype(jnp.float32), axis=1
    )
    mixed = jnp.dot(
        combine,
        summed.reshape(slot_count * capacity, model_width),
        precision=lax.Precision.HIGHEST,
        preferred_element_type=jnp.float32,
    )
    return mixed.astype(jnp.bfloat16)


def params(**kw):
    return pltpu.CompilerParams(vmem_limit_bytes=VMEM_BYTES, **kw)


VMEM = pl.BlockSpec(memory_space=pltpu.VMEM)
SMEM = pl.BlockSpec(memory_space=pltpu.SMEM)
HBM = pl.BlockSpec(memory_space=pl.ANY)


def cost(flops, size):
    return pl.CostEstimate(flops=int(flops), bytes_accessed=int(size), transcendentals=0)


def fold_matrix(groups):
    g, q, c = np.meshgrid(np.arange(groups), np.arange(FOLD), np.arange(CAP), indexing="ij")
    size = groups * FOLD * CAP
    matrix = np.zeros((size, size), np.float32)
    matrix[
        (q * groups * CAP + g * CAP + c).ravel(), (g * FOLD * CAP + q * CAP + c).ravel()
    ] = 1.0
    return matrix


def dispatch_kernel(widths, place_ref, experts_ref, replicas_ref, tokens_ref, base_ref, *pieces):
    tok = tokens_ref.shape[0]
    rows = pieces[0].shape[0]
    slots = rows // (FOLD * CAP)
    experts, replicas = experts_ref[...], replicas_ref[...]
    slot = jnp.zeros((1, tok), jnp.int32)
    for r in range(place_ref.shape[0]):
        for e in range(place_ref.shape[1]):
            slot = jnp.where((experts == e) & (replicas == r), place_ref[r, e], slot)
    hit = lax.broadcasted_iota(jnp.int32, (slots, tok), 0) == slot
    earlier = lax.broadcasted_iota(jnp.int32, (tok, tok), 0) < lax.broadcasted_iota(
        jnp.int32, (tok, tok), 1
    )
    before = jnp.dot(
        hit.astype(jnp.bfloat16), earlier.astype(jnp.bfloat16), preferred_element_type=jnp.float32
    )
    rank = jnp.sum(jnp.where(hit, before, 0.0), axis=0, keepdims=True).astype(jnp.int32)
    base = slot * (FOLD * CAP) + rank
    base_ref[...] = base
    row = lax.broadcasted_iota(jnp.int32, (rows, tok), 0)
    select = jnp.concatenate(
        [(row == base + q * CAP).astype(jnp.bfloat16) for q in range(FOLD)], axis=1
    )
    start = 0
    for piece, width in zip(pieces, widths):
        folded = jnp.concatenate(
            [tokens_ref[:, start + q * width : start + (q + 1) * width] for q in range(FOLD)],
            axis=0,
        )
        piece[...] = jnp.dot(select, folded, preferred_element_type=jnp.float32).astype(
            jnp.bfloat16
        )
        start += FOLD * width


def dispatch(placement, experts, replicas, tokens, slots):
    tok, model = tokens.shape
    rows = slots * FOLD * CAP
    out_shape = [jax.ShapeDtypeStruct((1, tok), jnp.int32)] + [
        jax.ShapeDtypeStruct((rows, width), jnp.bfloat16) for width in DISPATCH
    ]
    return pl.pallas_call(
        functools.partial(dispatch_kernel, DISPATCH),
        out_shape=out_shape,
        in_specs=[SMEM, VMEM, VMEM, VMEM],
        out_specs=[VMEM] * len(out_shape),
        compiler_params=params(),
        cost_estimate=cost(2 * rows * tok * model, 5 * tok * model),
        name="dispatch",
    )(placement.T, experts.reshape(1, tok), replicas.reshape(1, tok), tokens)


class Stream:
    def __init__(self, buffer, sems, tiles):
        self.buffer = buffer
        self.depth = buffer.shape[0]
        self.parts = []
        self.copies = []
        for n, tile in enumerate(tiles):
            slot = n % self.depth
            part = buffer.at[slot, pl.ds(0, tile.shape[0]), pl.ds(0, tile.shape[1])]
            self.parts.append(part)
            self.copies.append(pltpu.make_async_copy(tile, part, sems.at[slot]))
        self.begun = 0

    def ahead(self, upto):
        while self.begun < min(upto, len(self.copies)):
            self.copies[self.begun].start()
            self.begun += 1

    def take(self, n):
        self.copies[n].wait()
        return self.parts[n][...]

    def free(self, n):
        self.ahead(n + 1 + self.depth)


def unfold(block_ref, order_ref, x_ref):
    rows, width = x_ref.shape[0], block_ref.shape[1]
    value = jnp.dot(order_ref[...], block_ref[...], preferred_element_type=jnp.float32)
    value = value.astype(jnp.bfloat16)
    for q in range(FOLD):
        x_ref[:, q * width : (q + 1) * width] = value[q * rows : (q + 1) * rows]


def project(x_ref, tiles, totals, given):
    for n in range(x_ref.shape[1] // STEP):
        x = x_ref[:, n * STEP : (n + 1) * STEP]
        for m, total in enumerate(totals):
            value = jnp.dot(x, tiles.take(2 * n + m), preferred_element_type=jnp.float32)
            if n > 0:
                value = total[...] + value
            elif given is not None:
                value = given[m][...] + value
            total[...] = value
            tiles.free(2 * n + m)


def in_tiles(wg_ref, wu_ref, start, count):
    return [
        w.at[0, pl.ds(start + n * STEP, STEP)] for n in range(count) for w in (wg_ref, wu_ref)
    ]


def first_kernel(start, order_ref, block_ref, wg_ref, wu_ref, accg_ref, accu_ref, x_ref, w_ref, sem):
    tiles = Stream(w_ref, sem, in_tiles(wg_ref, wu_ref, start, x_ref.shape[1] // STEP))
    tiles.ahead(tiles.depth)
    unfold(block_ref, order_ref, x_ref)
    project(x_ref, tiles, (accg_ref, accu_ref), None)


def first_part(order, block, gate_weight, up_weight, start):
    rows = block.shape[0] // FOLD
    model, hidden = FOLD * block.shape[1], gate_weight.shape[2]
    acc = jax.ShapeDtypeStruct((rows, hidden), jnp.float32)
    return pl.pallas_call(
        functools.partial(first_kernel, start),
        out_shape=[acc, acc],
        in_specs=[VMEM, VMEM, HBM, HBM],
        out_specs=[VMEM, VMEM],
        scratch_shapes=[
            pltpu.VMEM((rows, model), jnp.bfloat16),
            pltpu.VMEM((DEPTH, STEP, hidden), jnp.bfloat16),
            pltpu.SemaphoreType.DMA((DEPTH,)),
        ],
        compiler_params=params(),
        cost_estimate=cost(4 * rows * model * hidden, 4 * model * hidden),
        name="first_part",
    )(order, block, gate_weight, up_weight)


def second_kernel(
    start,
    order_ref,
    back_ref,
    block_ref,
    ing_ref,
    inu_ref,
    wg_ref,
    wu_ref,
    wd_ref,
    out_ref,
    x_ref,
    accg_ref,
    accu_ref,
    hidden_ref,
    w_ref,
    d_ref,
    sem,
    dsem,
):
    width = out_ref.shape[1]
    spans = [(j, min(BACK_COLUMNS, width - j)) for j in range(0, width, BACK_COLUMNS)]
    tiles = Stream(w_ref, sem, in_tiles(wg_ref, wu_ref, start, x_ref.shape[1] // STEP))
    outs = Stream(
        d_ref,
        dsem,
        [wd_ref.at[0, :, pl.ds(q * width + j, w)] for j, w in spans for q in range(FOLD)],
    )
    tiles.ahead(tiles.depth)
    outs.ahead(outs.depth)
    unfold(block_ref, order_ref, x_ref)
    project(x_ref, tiles, (accg_ref, accu_ref), (ing_ref, inu_ref))
    gate_val = accg_ref[...]
    hidden_ref[...] = (gate_val / (1.0 + jnp.exp(-gate_val)) * accu_ref[...]).astype(jnp.bfloat16)
    for i, (j, w) in enumerate(spans):
        values = []
        for n in range(i * FOLD, (i + 1) * FOLD):
            value = jnp.dot(hidden_ref[...], outs.take(n), preferred_element_type=jnp.float32)
            values.append(value.astype(jnp.bfloat16))
            outs.free(n)
        out_ref[:, j : j + w] = jnp.dot(
            back_ref[...], jnp.concatenate(values, axis=0), preferred_element_type=jnp.float32
        ).astype(jnp.bfloat16)


def second_part(order, back, block, accs, gate_weight, up_weight, down_weight, start):
    rows = block.shape[0] // FOLD
    model, hidden, whole = FOLD * block.shape[1], down_weight.shape[1], down_weight.shape[2]
    return pl.pallas_call(
        functools.partial(second_kernel, start),
        out_shape=jax.ShapeDtypeStruct((block.shape[0], whole // FOLD), jnp.bfloat16),
        in_specs=[VMEM] * 5 + [HBM] * 3,
        out_specs=VMEM,
        scratch_shapes=[
            pltpu.VMEM((rows, model), jnp.bfloat16),
            pltpu.VMEM((rows, hidden), jnp.float32),
            pltpu.VMEM((rows, hidden), jnp.float32),
            pltpu.VMEM((rows, hidden), jnp.bfloat16),
            pltpu.VMEM((2 * model // STEP, STEP, hidden), jnp.bfloat16),
            pltpu.VMEM((DEPTH, hidden, BACK_COLUMNS), jnp.bfloat16),
            pltpu.SemaphoreType.DMA((2 * model // STEP,)),
            pltpu.SemaphoreType.DMA((DEPTH,)),
        ],
        compiler_params=params(),
        cost_estimate=cost(
            2 * rows * (2 * model + whole) * hidden, 2 * (2 * model + whole) * hidden
        ),
        name="second_part",
    )(order, back, block, *accs, gate_weight, up_weight, down_weight)


def column(row):
    n = row.shape[1]
    eye = lax.broadcasted_iota(jnp.int32, (n, n), 0) == lax.broadcasted_iota(jnp.int32, (n, n), 1)
    return jnp.sum(jnp.where(eye, row, jnp.zeros_like(row)), axis=1, keepdims=True)


def finish_kernel(base_ref, gates_ref, *refs):
    pieces, out_ref = refs[:-1], refs[-1]
    base = column(base_ref[...])
    gate = column(gates_ref[...])
    lane = lax.broadcasted_iota(jnp.int32, (base.shape[0], pieces[0].shape[0]), 1)
    select = [(lane == base + q * CAP).astype(jnp.bfloat16) for q in range(FOLD)]
    start = 0
    for piece in pieces:
        width = piece.shape[1]
        for q in range(FOLD):
            value = jnp.dot(select[q], piece[...], preferred_element_type=jnp.float32)
            out_ref[:, start : start + width] = (gate * value).astype(jnp.bfloat16)
            start += width


def finish(base, gates, pieces):
    tok = base.shape[1]
    model = FOLD * sum(p.shape[1] for p in pieces)
    return pl.pallas_call(
        finish_kernel,
        out_shape=jax.ShapeDtypeStruct((tok, model), jnp.bfloat16),
        in_specs=[VMEM] * (2 + len(pieces)),
        out_specs=VMEM,
        compiler_params=params(),
        cost_estimate=cost(2 * tok * model * 384, 5 * tok * model),
        name="finish",
    )(base, gates.reshape(1, tok), *pieces)


def swap(block, slots):
    rows, width = block.shape
    out = lax.all_to_all(
        block.reshape(slots, rows // slots, width),
        ("node", "local"),
        split_axis=0,
        concat_axis=0,
        tiled=True,
    )
    return out.reshape(rows, width)


def per_device_folded(
    tokens, experts, replicas, gates, placement, gate_weight, up_weight, down_weight
):
    slots = lax.axis_size(("node", "local"))
    matrix = fold_matrix(slots)
    order = jnp.asarray(matrix, jnp.bfloat16)
    back = jnp.asarray(matrix.T, jnp.bfloat16)
    base, *pieces = dispatch(placement, experts, replicas, tokens, slots)
    early = swap(pieces[0], slots)
    late, _ = lax.optimization_barrier((pieces[1], early))
    late = swap(late, slots)
    accs = first_part(order, early, gate_weight, up_weight, 0)
    start = FOLD * DISPATCH[0]
    results = second_part(order, back, late, accs, gate_weight, up_weight, down_weight, start)
    return finish(base, gates, [swap(results, slots)])


def solution(mesh):
    in_specs = (
        P(("parts", "node", "local"), None),
        P(("parts", "node", "local"), None),
        P(("parts", "node", "local"), None),
        P(("parts", "node", "local"), None),
        P(),
        P(("node", "local"), None, None),
        P(("node", "local"), None, None),
        P(("node", "local"), None, None),
    )
    out_specs = P(("parts", "node", "local"), None)

    def per_device(*args):
        folded = (
            mesh.shape["node"] * mesh.shape["local"] == 16
            and args[1].shape[1] == 1
            and args[5].shape[2] == FF
            and args[0].shape[1] == FOLD * sum(DISPATCH)
        )
        return (per_device_folded if folded else per_device_general)(*args)

    return jax.shard_map(
        per_device, mesh=mesh, in_specs=in_specs, out_specs=out_specs, check_vma=False
    )
```

```python
import functools

import jax
import jax.numpy as jnp
import numpy as np
from jax import lax
from jax.experimental import pallas as pl
from jax.experimental.pallas import tpu as pltpu
from jax.sharding import PartitionSpec as P

FF = 2048
CAP = 6
FOLD = 4
STEP = 512
FLIGHT = 4
DEPTH = 6
HOPS = (1, 2, 4, 6, 5, 7, 3)
LAG = 3
DISPATCH = (896, 896)
BACK_COLUMNS = 512
VMEM_BYTES = 56 * 1024 * 1024


def route_tables(experts, replicas, gates, placement, slot_count, capacity):
    expert_hit = (
        experts[:, :, None] == jnp.arange(placement.shape[0], dtype=jnp.int32)[None, None, :]
    )
    replica_hit = (
        replicas[:, :, None] == jnp.arange(placement.shape[1], dtype=jnp.int32)[None, None, :]
    )
    joined = expert_hit[:, :, :, None] & replica_hit[:, :, None, :]
    slot_ids = jnp.sum(jnp.where(joined, placement[None, None, :, :], 0), axis=(2, 3))
    flat_slots = slot_ids.reshape(-1)
    slot_hit = (flat_slots[:, None] == jnp.arange(slot_count, dtype=jnp.int32)[None, :]).astype(
        jnp.int32
    )
    before = jnp.cumsum(slot_hit, axis=0) - slot_hit
    rank = jnp.sum(slot_hit * before, axis=1)
    position = (flat_slots * capacity + rank).reshape(slot_ids.shape)
    grid = position[:, :, None] == jnp.arange(slot_count * capacity, dtype=jnp.int32)[None, None, :]
    scatter = jnp.any(grid, axis=1).T
    zero_gate = jnp.zeros_like(gates)[:, :, None]
    combine = jnp.sum(jnp.where(grid, gates[:, :, None], zero_gate), axis=1)
    return (scatter, combine)


def per_device_general(
    tokens, experts, replicas, gates, placement, gate_weight, up_weight, down_weight
):
    model_width = tokens.shape[1]
    hidden_dev = gate_weight.shape[2]
    group_size = FF // hidden_dev
    devices_all = lax.axis_size(("node", "local"))
    slot_count = devices_all // group_size
    capacity = CAP
    scatter, combine = route_tables(experts, replicas, gates, placement, slot_count, capacity)
    outgoing = jnp.dot(
        scatter.astype(jnp.bfloat16), tokens, preferred_element_type=jnp.float32
    ).astype(jnp.bfloat16)
    outgoing = outgoing.reshape(slot_count, capacity, model_width)
    sending = jnp.repeat(outgoing, group_size, axis=0)
    arrived = lax.all_to_all(sending, ("node", "local"), split_axis=0, concat_axis=0, tiled=True)
    row_block = arrived.reshape(-1, model_width)
    gate_val = jnp.dot(row_block, gate_weight[0], preferred_element_type=jnp.float32)
    up_val = jnp.dot(row_block, up_weight[0], preferred_element_type=jnp.float32)
    hidden = (jax.nn.silu(gate_val) * up_val).astype(jnp.bfloat16)
    partial_value = (
        jnp.dot(hidden, down_weight[0], preferred_element_type=jnp.float32)
        .astype(jnp.bfloat16)
        .reshape(arrived.shape)
    )
    returned = lax.all_to_all(
        partial_value, ("node", "local"), split_axis=0, concat_axis=0, tiled=True
    )
    summed = jnp.sum(
        returned.reshape(slot_count, group_size, capacity, model_width).astype(jnp.float32), axis=1
    )
    mixed = jnp.dot(
        combine,
        summed.reshape(slot_count * capacity, model_width),
        precision=lax.Precision.HIGHEST,
        preferred_element_type=jnp.float32,
    )
    return mixed.astype(jnp.bfloat16)


def params(size=VMEM_BYTES):
    return pltpu.CompilerParams(vmem_limit_bytes=size)


VMEM = pl.BlockSpec(memory_space=pltpu.VMEM)
SMEM = pl.BlockSpec(memory_space=pltpu.SMEM)
HBM = pl.BlockSpec(memory_space=pl.ANY)


def cost(flops, size):
    return pl.CostEstimate(flops=int(flops), bytes_accessed=int(size), transcendentals=0)


def fold_matrix(groups):
    g, q, c = np.meshgrid(np.arange(groups), np.arange(FOLD), np.arange(CAP), indexing="ij")
    size = groups * FOLD * CAP
    matrix = np.zeros((size, size), np.float32)
    matrix[
        (q * groups * CAP + g * CAP + c).ravel(), (g * FOLD * CAP + q * CAP + c).ravel()
    ] = 1.0
    return matrix


def fold_table(n_local):
    q, k, b, c = np.meshgrid(
        np.arange(FOLD), np.arange(n_local), np.arange(2), np.arange(CAP), indexing="ij"
    )
    table = np.zeros((8, q.size), np.int32)
    table[0], table[1], table[2] = k.ravel(), b.ravel(), (q * CAP + c).ravel()
    return table


def dispatch_kernel(n_local, place_ref, own_pick, mate_pick, own_ref, mate_ref, spot_ref, *blocks):
    tok = own_ref.shape[0]
    both = 2 * tok
    node, local = lax.axis_index("node"), lax.axis_index("local")
    slots = 2 * n_local
    pick = jnp.concatenate([own_pick[...], mate_pick[...]], axis=1)
    slot = jnp.zeros((1, both), jnp.int32)
    columns = place_ref.shape[0]
    for e in range(place_ref.shape[1]):
        for r in range(columns):
            slot = jnp.where(pick == e * columns + r, place_ref[r, e], slot)
    hit = lax.broadcasted_iota(jnp.int32, (slots, both), 0) == slot
    early = lax.broadcasted_iota(jnp.int32, (both, both), 0)
    late = lax.broadcasted_iota(jnp.int32, (both, both), 1)
    earlier = (early < late) & ((early >= tok) == (late >= tok))
    before = jnp.dot(
        hit.astype(jnp.bfloat16), earlier.astype(jnp.bfloat16), preferred_element_type=jnp.float32
    )
    rank = jnp.sum(jnp.where(hit, before, 0.0), axis=0, keepdims=True).astype(jnp.int32)
    there = slot - node * n_local
    hop = there ^ local
    second = (lax.broadcasted_iota(jnp.int32, (1, both), 1) >= tok).astype(jnp.int32)
    base = jnp.where(
        (there >= 0) & (there < n_local), (hop * 2 + second) * (FOLD * CAP) + rank, -FOLD * CAP
    )
    spot_ref[...] = (slot * (FOLD * CAP) + rank)[:, :tok]
    size = 2 * FOLD * CAP
    row = lax.broadcasted_iota(jnp.int32, (n_local * size, both), 0)
    select = jnp.concatenate(
        [(row == base + q * CAP).astype(jnp.bfloat16) for q in range(FOLD)], axis=1
    )
    start = 0
    for piece, width in enumerate(DISPATCH):
        folded = jnp.concatenate(
            [
                ref[:, start + q * width : start + (q + 1) * width]
                for q in range(FOLD)
                for ref in (own_ref, mate_ref)
            ],
            axis=0,
        )
        value = jnp.dot(select, folded, preferred_element_type=jnp.float32).astype(jnp.bfloat16)
        for hop_id in range(n_local):
            blocks[piece * n_local + hop_id][...] = value[hop_id * size : (hop_id + 1) * size]
        start += FOLD * width


def dispatch(placement, own_pick, mate_pick, own, mate, n_local):
    tok, model = own.shape
    size = 2 * FOLD * CAP
    out_shape = [jax.ShapeDtypeStruct((1, tok), jnp.int32)] + [
        jax.ShapeDtypeStruct((size, width), jnp.bfloat16)
        for width in DISPATCH
        for _ in range(n_local)
    ]
    outs = pl.pallas_call(
        functools.partial(dispatch_kernel, n_local),
        out_shape=out_shape,
        in_specs=[SMEM, VMEM, VMEM, VMEM, VMEM],
        out_specs=[VMEM] * len(out_shape),
        compiler_params=params(),
        cost_estimate=cost(4 * n_local * size * tok * model, 10 * tok * model),
        name="dispatch",
    )(placement.T, own_pick, mate_pick, own, mate)
    return outs[0], [outs[1 + i * n_local : 1 + (i + 1) * n_local] for i in range(len(DISPATCH))]


class Stream:
    def __init__(self, *kinds):
        self.parts = []
        self.copies = []
        for buffer, sems, tiles in kinds:
            for n, tile in enumerate(tiles):
                slot = n % buffer.shape[0]
                part = buffer.at[slot, pl.ds(0, tile.shape[0]), pl.ds(0, tile.shape[1])]
                self.parts.append(part)
                self.copies.append(pltpu.make_async_copy(tile, part, sems.at[slot]))
        self.taken = 0
        for copy in self.copies[:FLIGHT]:
            copy.start()

    def take(self):
        n = self.taken
        self.copies[n].wait()
        if n + FLIGHT < len(self.copies):
            self.copies[n + FLIGHT].start()
        self.taken += 1
        return self.parts[n][...]


def unfold(blocks, order_ref, x_ref):
    rows, width = x_ref.shape[0], blocks[0].shape[1]
    folded = jnp.concatenate([b[...] for b in blocks], axis=0)
    value = jnp.dot(order_ref[...], folded, preferred_element_type=jnp.float32)
    value = value.astype(jnp.bfloat16)
    for q in range(FOLD):
        x_ref[:, q * width : (q + 1) * width] = value[q * rows : (q + 1) * rows]


def project(x_ref, tiles, totals, given):
    for n in range(x_ref.shape[1] // STEP):
        x = x_ref[:, n * STEP : (n + 1) * STEP]
        for m, total in enumerate(totals):
            value = jnp.dot(x, tiles.take(), preferred_element_type=jnp.float32)
            if n > 0:
                value = total[...] + value
            elif given is not None:
                value = given[m][...] + value
            total[...] = value


def in_tiles(wg_ref, wu_ref, start, count):
    return [
        w.at[0, pl.ds(start + n * STEP, STEP)] for n in range(count) for w in (wg_ref, wu_ref)
    ]


def first_kernel(n_local, start, order_ref, *refs):
    blocks = refs[:n_local]
    wg_ref, wu_ref, accg_ref, accu_ref, x_ref, w_ref, sem = refs[n_local:]
    tiles = Stream((w_ref, sem, in_tiles(wg_ref, wu_ref, start, x_ref.shape[1] // STEP)))
    unfold(blocks, order_ref, x_ref)
    project(x_ref, tiles, (accg_ref, accu_ref), None)


def first_part(order, blocks, gate_weight, up_weight, start):
    n_local = len(blocks)
    rows = 2 * n_local * CAP
    model, hidden = FOLD * blocks[0].shape[1], gate_weight.shape[2]
    acc = jax.ShapeDtypeStruct((rows, hidden), jnp.float32)
    return pl.pallas_call(
        functools.partial(first_kernel, n_local, start),
        out_shape=[acc, acc],
        in_specs=[VMEM] * (1 + n_local) + [HBM] * 2,
        out_specs=[VMEM, VMEM],
        scratch_shapes=[
            pltpu.VMEM((rows, model), jnp.bfloat16),
            pltpu.VMEM((DEPTH, STEP, hidden), jnp.bfloat16),
            pltpu.SemaphoreType.DMA((DEPTH,)),
        ],
        compiler_params=params(),
        cost_estimate=cost(4 * rows * model * hidden, 4 * model * hidden),
        name="first_part",
    )(order, *blocks, gate_weight, up_weight)


def second_kernel(n_local, start, order_ref, table_ref, *refs):
    blocks, refs = refs[:n_local], refs[n_local:]
    ing_ref, inu_ref, wg_ref, wu_ref, wd_ref, out_ref = refs[:6]
    x_ref, accg_ref, accu_ref, hidden_ref, w_ref, d_ref, sem, dsem = refs[6:]
    width = out_ref.shape[1]
    spans = [(j, min(BACK_COLUMNS, width - j)) for j in range(0, width, BACK_COLUMNS)]
    out_tiles = [wd_ref.at[0, :, pl.ds(q * width + j, w)] for j, w in spans for q in range(FOLD)]
    tiles = Stream(
        (w_ref, sem, in_tiles(wg_ref, wu_ref, start, x_ref.shape[1] // STEP)),
        (d_ref, dsem, out_tiles),
    )
    node, local = lax.axis_index("node"), lax.axis_index("local")
    device = (table_ref[1:2, :] ^ node) * n_local + (table_ref[0:1, :] ^ local)
    target = device * (FOLD * CAP) + table_ref[2:3, :]
    size = target.shape[1]
    back = (lax.broadcasted_iota(jnp.int32, (size, size), 0) == target).astype(jnp.bfloat16)
    unfold(blocks, order_ref, x_ref)
    project(x_ref, tiles, (accg_ref, accu_ref), (ing_ref, inu_ref))
    gate_val = accg_ref[...]
    hidden_ref[...] = (gate_val / (1.0 + jnp.exp(-gate_val)) * accu_ref[...]).astype(jnp.bfloat16)
    for j, w in spans:
        values = []
        for _ in range(FOLD):
            value = jnp.dot(hidden_ref[...], tiles.take(), preferred_element_type=jnp.float32)
            values.append(value.astype(jnp.bfloat16))
        out_ref[:, j : j + w] = jnp.dot(
            back, jnp.concatenate(values, axis=0), preferred_element_type=jnp.float32
        ).astype(jnp.bfloat16)


def second_part(order, table, blocks, accs, gate_weight, up_weight, down_weight, start):
    n_local = len(blocks)
    rows = 2 * n_local * CAP
    model, hidden, whole = FOLD * blocks[0].shape[1], down_weight.shape[1], down_weight.shape[2]
    return pl.pallas_call(
        functools.partial(second_kernel, n_local, start),
        out_shape=jax.ShapeDtypeStruct((rows * FOLD, whole // FOLD), jnp.bfloat16),
        in_specs=[VMEM] * (4 + n_local) + [HBM] * 3,
        out_specs=VMEM,
        scratch_shapes=[
            pltpu.VMEM((rows, model), jnp.bfloat16),
            pltpu.VMEM((rows, hidden), jnp.float32),
            pltpu.VMEM((rows, hidden), jnp.float32),
            pltpu.VMEM((rows, hidden), jnp.bfloat16),
            pltpu.VMEM((DEPTH, STEP, hidden), jnp.bfloat16),
            pltpu.VMEM((DEPTH, hidden, BACK_COLUMNS), jnp.bfloat16),
            pltpu.SemaphoreType.DMA((DEPTH,)),
            pltpu.SemaphoreType.DMA((DEPTH,)),
        ],
        compiler_params=params(),
        cost_estimate=cost(
            2 * rows * (2 * model + whole) * hidden, 2 * (2 * model + whole) * hidden
        ),
        name="second_part",
    )(order, table, *blocks, *accs, gate_weight, up_weight, down_weight)


def column(row):
    n = row.shape[1]
    eye = lax.broadcasted_iota(jnp.int32, (n, n), 0) == lax.broadcasted_iota(jnp.int32, (n, n), 1)
    return jnp.sum(jnp.where(eye, row, jnp.zeros_like(row)), axis=1, keepdims=True)


def finish_kernel(base_ref, gates_ref, *refs):
    pieces, out_ref = refs[:-1], refs[-1]
    base = column(base_ref[...])
    gate = column(gates_ref[...])
    lane = lax.broadcasted_iota(jnp.int32, (base.shape[0], pieces[0].shape[0]), 1)
    select = [(lane == base + q * CAP).astype(jnp.bfloat16) for q in range(FOLD)]
    start = 0
    for piece in pieces:
        width = piece.shape[1]
        for q in range(FOLD):
            value = jnp.dot(select[q], piece[...], preferred_element_type=jnp.float32)
            out_ref[:, start : start + width] = (gate * value).astype(jnp.bfloat16)
            start += width


def finish(base, gates, pieces):
    tok = base.shape[1]
    model = FOLD * sum(p.shape[1] for p in pieces)
    return pl.pallas_call(
        finish_kernel,
        out_shape=jax.ShapeDtypeStruct((tok, model), jnp.bfloat16),
        in_specs=[VMEM] * (2 + len(pieces)),
        out_specs=VMEM,
        compiler_params=params(8 * 1024 * 1024),
        cost_estimate=cost(2 * tok * model * 384, 5 * tok * model),
        name="finish",
    )(base, gates.reshape(1, tok), *pieces)


def swap(block, slots):
    rows, width = block.shape
    out = lax.all_to_all(
        block.reshape(slots, rows // slots, width),
        ("node", "local"),
        split_axis=0,
        concat_axis=0,
        tiled=True,
    )
    return out.reshape(rows, width)


def swap_hops(blocks, after=None):
    n_local = len(blocks)
    out = list(blocks)
    for n, hop in enumerate(HOPS):
        block = blocks[hop]
        if after is not None:
            earlier = after[HOPS[min(n + LAG, len(HOPS) - 1)]]
            block, _ = lax.optimization_barrier((block, earlier))
        out[hop] = lax.ppermute(block, "local", [(i, i ^ hop) for i in range(n_local)])
    return out


def swap_mate(value):
    return lax.ppermute(value, "node", [(0, 1), (1, 0)])


def per_device_folded(
    tokens, experts, replicas, gates, placement, gate_weight, up_weight, down_weight
):
    tok = tokens.shape[0]
    n_local = lax.axis_size("local")
    slots = 2 * n_local
    order = jnp.asarray(fold_matrix(slots), jnp.bfloat16)
    table = jnp.asarray(fold_table(n_local))
    mate = swap_mate(tokens)
    pick = (experts * placement.shape[1] + replicas).reshape(1, tok)
    spot, pieces = dispatch(placement, pick, swap_mate(pick), tokens, mate, n_local)
    early = swap_hops(pieces[0])
    late = swap_hops(pieces[1], early)
    accs = first_part(order, early, gate_weight, up_weight, 0)
    start = FOLD * DISPATCH[0]
    results = second_part(order, table, late, accs, gate_weight, up_weight, down_weight, start)
    return finish(spot, gates, [swap(results, slots)])


def solution(mesh):
    in_specs = (
        P(("parts", "node", "local"), None),
        P(("parts", "node", "local"), None),
        P(("parts", "node", "local"), None),
        P(("parts", "node", "local"), None),
        P(),
        P(("node", "local"), None, None),
        P(("node", "local"), None, None),
        P(("node", "local"), None, None),
    )
    out_specs = P(("parts", "node", "local"), None)

    def per_device(*args):
        folded = (
            mesh.shape["node"] == 2
            and mesh.shape["local"] == 8
            and args[1].shape[1] == 1
            and args[5].shape[2] == FF
            and args[0].shape[1] == FOLD * sum(DISPATCH)
        )
        return (per_device_folded if folded else per_device_general)(*args)

    return jax.shard_map(
        per_device, mesh=mesh, in_specs=in_specs, out_specs=out_specs, check_vma=False
    )
```

```python
import functools

import jax
import jax.numpy as jnp
from jax import lax
from jax.experimental import pallas as pl
from jax.experimental.pallas import tpu as pltpu
from jax.sharding import PartitionSpec as P

FF = 2048
CAP = 6
FOLD = 4
STEP = 512
FLIGHT = 4
DEPTH = 6
HOPS = (1, 2, 4, 6, 5, 7, 3)
LAG = 3
DISPATCH = (896, 896)
BACK_COLUMNS = 512
VMEM_BYTES = 40 * 1024 * 1024


def route_tables(experts, replicas, gates, placement, slot_count, capacity):
    expert_hit = (
        experts[:, :, None] == jnp.arange(placement.shape[0], dtype=jnp.int32)[None, None, :]
    )
    replica_hit = (
        replicas[:, :, None] == jnp.arange(placement.shape[1], dtype=jnp.int32)[None, None, :]
    )
    joined = expert_hit[:, :, :, None] & replica_hit[:, :, None, :]
    slot_ids = jnp.sum(jnp.where(joined, placement[None, None, :, :], 0), axis=(2, 3))
    flat_slots = slot_ids.reshape(-1)
    slot_hit = (flat_slots[:, None] == jnp.arange(slot_count, dtype=jnp.int32)[None, :]).astype(
        jnp.int32
    )
    before = jnp.cumsum(slot_hit, axis=0) - slot_hit
    rank = jnp.sum(slot_hit * before, axis=1)
    position = (flat_slots * capacity + rank).reshape(slot_ids.shape)
    grid = position[:, :, None] == jnp.arange(slot_count * capacity, dtype=jnp.int32)[None, None, :]
    scatter = jnp.any(grid, axis=1).T
    zero_gate = jnp.zeros_like(gates)[:, :, None]
    combine = jnp.sum(jnp.where(grid, gates[:, :, None], zero_gate), axis=1)
    return (scatter, combine)


def per_device_general(
    tokens, experts, replicas, gates, placement, gate_weight, up_weight, down_weight
):
    model_width = tokens.shape[1]
    hidden_dev = gate_weight.shape[2]
    group_size = FF // hidden_dev
    devices_all = lax.axis_size(("node", "local"))
    slot_count = devices_all // group_size
    capacity = CAP
    scatter, combine = route_tables(experts, replicas, gates, placement, slot_count, capacity)
    outgoing = jnp.dot(
        scatter.astype(jnp.bfloat16), tokens, preferred_element_type=jnp.float32
    ).astype(jnp.bfloat16)
    outgoing = outgoing.reshape(slot_count, capacity, model_width)
    sending = jnp.repeat(outgoing, group_size, axis=0)
    arrived = lax.all_to_all(sending, ("node", "local"), split_axis=0, concat_axis=0, tiled=True)
    row_block = arrived.reshape(-1, model_width)
    gate_val = jnp.dot(row_block, gate_weight[0], preferred_element_type=jnp.float32)
    up_val = jnp.dot(row_block, up_weight[0], preferred_element_type=jnp.float32)
    hidden = (jax.nn.silu(gate_val) * up_val).astype(jnp.bfloat16)
    partial_value = (
        jnp.dot(hidden, down_weight[0], preferred_element_type=jnp.float32)
        .astype(jnp.bfloat16)
        .reshape(arrived.shape)
    )
    returned = lax.all_to_all(
        partial_value, ("node", "local"), split_axis=0, concat_axis=0, tiled=True
    )
    summed = jnp.sum(
        returned.reshape(slot_count, group_size, capacity, model_width).astype(jnp.float32), axis=1
    )
    mixed = jnp.dot(
        combine,
        summed.reshape(slot_count * capacity, model_width),
        precision=lax.Precision.HIGHEST,
        preferred_element_type=jnp.float32,
    )
    return mixed.astype(jnp.bfloat16)


def params(size=VMEM_BYTES):
    return pltpu.CompilerParams(vmem_limit_bytes=size)


VMEM = pl.BlockSpec(memory_space=pltpu.VMEM)
SMEM = pl.BlockSpec(memory_space=pltpu.SMEM)
HBM = pl.BlockSpec(memory_space=pl.ANY)


def cost(flops, size):
    return pl.CostEstimate(flops=int(flops), bytes_accessed=int(size), transcendentals=0)


def unpack_row(row, groups):
    part = jnp.zeros_like(row)
    for q in range(1, FOLD):
        part = part + (row >= q * groups * CAP).astype(jnp.int32)
    place = row - part * (groups * CAP)
    group = ((place.astype(jnp.float32) + 0.5) * (1.0 / CAP)).astype(jnp.int32)
    return group, part * CAP + place - group * CAP


def dispatch_kernel(n_local, place_ref, own_pick, mate_pick, own_ref, mate_ref, spot_ref, *blocks):
    tok = own_ref.shape[0]
    both = 2 * tok
    node, local = lax.axis_index("node"), lax.axis_index("local")
    slots = 2 * n_local
    pick = jnp.concatenate([own_pick[...], mate_pick[...]], axis=1)
    slot = jnp.zeros((1, both), jnp.int32)
    columns = place_ref.shape[0]
    for e in range(place_ref.shape[1]):
        for r in range(columns):
            slot = jnp.where(pick == e * columns + r, place_ref[r, e], slot)
    hit = lax.broadcasted_iota(jnp.int32, (slots, both), 0) == slot
    early = lax.broadcasted_iota(jnp.int32, (both, both), 0)
    late = lax.broadcasted_iota(jnp.int32, (both, both), 1)
    earlier = (early < late) & ((early >= tok) == (late >= tok))
    before = jnp.dot(
        hit.astype(jnp.bfloat16), earlier.astype(jnp.bfloat16), preferred_element_type=jnp.float32
    )
    rank = jnp.sum(jnp.where(hit, before, 0.0), axis=0, keepdims=True).astype(jnp.int32)
    there = slot - node * n_local
    hop = there ^ local
    second = (lax.broadcasted_iota(jnp.int32, (1, both), 1) >= tok).astype(jnp.int32)
    base = jnp.where(
        (there >= 0) & (there < n_local), (hop * 2 + second) * (FOLD * CAP) + rank, -FOLD * CAP
    )
    spot_ref[...] = (slot * (FOLD * CAP) + rank)[:, :tok]
    size = 2 * FOLD * CAP
    row = lax.broadcasted_iota(jnp.int32, (n_local * size, both), 0)
    select = jnp.concatenate(
        [(row == base + q * CAP).astype(jnp.bfloat16) for q in range(FOLD)], axis=1
    )
    start = 0
    for piece, width in enumerate(DISPATCH):
        folded = jnp.concatenate(
            [
                ref[:, start + q * width : start + (q + 1) * width]
                for q in range(FOLD)
                for ref in (own_ref, mate_ref)
            ],
            axis=0,
        )
        value = jnp.dot(select, folded, preferred_element_type=jnp.float32).astype(jnp.bfloat16)
        for hop_id in range(n_local):
            blocks[piece * n_local + hop_id][...] = value[hop_id * size : (hop_id + 1) * size]
        start += FOLD * width


def dispatch(placement, own_pick, mate_pick, own, mate, n_local):
    tok, model = own.shape
    size = 2 * FOLD * CAP
    out_shape = [jax.ShapeDtypeStruct((1, tok), jnp.int32)] + [
        jax.ShapeDtypeStruct((size, width), jnp.bfloat16)
        for width in DISPATCH
        for _ in range(n_local)
    ]
    outs = pl.pallas_call(
        functools.partial(dispatch_kernel, n_local),
        out_shape=out_shape,
        in_specs=[SMEM, VMEM, VMEM, VMEM, VMEM],
        out_specs=[VMEM] * len(out_shape),
        compiler_params=params(),
        cost_estimate=cost(4 * n_local * size * tok * model, 10 * tok * model),
        name="dispatch",
    )(placement.T, own_pick, mate_pick, own, mate)
    return outs[0], [outs[1 + i * n_local : 1 + (i + 1) * n_local] for i in range(len(DISPATCH))]


class Stream:
    def __init__(self, *kinds):
        self.parts = []
        self.copies = []
        for buffer, sems, tiles in kinds:
            for n, tile in enumerate(tiles):
                slot = n % buffer.shape[0]
                part = buffer.at[slot, pl.ds(0, tile.shape[0]), pl.ds(0, tile.shape[1])]
                self.parts.append(part)
                self.copies.append(pltpu.make_async_copy(tile, part, sems.at[slot]))
        self.taken = 0
        for copy in self.copies[:FLIGHT]:
            copy.start()

    def take(self):
        n = self.taken
        self.copies[n].wait()
        if n + FLIGHT < len(self.copies):
            self.copies[n + FLIGHT].start()
        self.taken += 1
        return self.parts[n][...]


def unfold(blocks, x_ref):
    rows, width = x_ref.shape[0], blocks[0].shape[1]
    size = rows * FOLD
    group, inner = unpack_row(lax.broadcasted_iota(jnp.int32, (size, size), 0), rows // CAP)
    order = lax.broadcasted_iota(jnp.int32, (size, size), 1) == group * (FOLD * CAP) + inner
    folded = jnp.concatenate([b[...] for b in blocks], axis=0)
    value = jnp.dot(order.astype(jnp.bfloat16), folded, preferred_element_type=jnp.float32)
    value = value.astype(jnp.bfloat16)
    for q in range(FOLD):
        x_ref[:, q * width : (q + 1) * width] = value[q * rows : (q + 1) * rows]


def project(x_ref, tiles, totals, given):
    for n in range(x_ref.shape[1] // STEP):
        x = x_ref[:, n * STEP : (n + 1) * STEP]
        for m, total in enumerate(totals):
            value = jnp.dot(x, tiles.take(), preferred_element_type=jnp.float32)
            if n > 0:
                value = total[...] + value
            elif given is not None:
                value = given[m][...] + value
            total[...] = value


def in_tiles(wg_ref, wu_ref, start, count):
    return [
        w.at[0, pl.ds(start + n * STEP, STEP)] for n in range(count) for w in (wg_ref, wu_ref)
    ]


def first_kernel(n_local, start, *refs):
    blocks = refs[:n_local]
    wg_ref, wu_ref, accg_ref, accu_ref, x_ref, w_ref, sem = refs[n_local:]
    tiles = Stream((w_ref, sem, in_tiles(wg_ref, wu_ref, start, x_ref.shape[1] // STEP)))
    unfold(blocks, x_ref)
    project(x_ref, tiles, (accg_ref, accu_ref), None)


def first_part(blocks, gate_weight, up_weight, start):
    n_local = len(blocks)
    rows = 2 * n_local * CAP
    model, hidden = FOLD * blocks[0].shape[1], gate_weight.shape[2]
    acc = jax.ShapeDtypeStruct((rows, hidden), jnp.float32)
    return pl.pallas_call(
        functools.partial(first_kernel, n_local, start),
        out_shape=[acc, acc],
        in_specs=[VMEM] * n_local + [HBM] * 2,
        out_specs=[VMEM, VMEM],
        scratch_shapes=[
            pltpu.VMEM((rows, model), jnp.bfloat16),
            pltpu.VMEM((DEPTH, STEP, hidden), jnp.bfloat16),
            pltpu.SemaphoreType.DMA((DEPTH,)),
        ],
        compiler_params=params(),
        cost_estimate=cost(4 * rows * model * hidden, 4 * model * hidden),
        name="first_part",
    )(*blocks, gate_weight, up_weight)


def second_kernel(n_local, start, *refs):
    blocks, refs = refs[:n_local], refs[n_local:]
    ing_ref, inu_ref, wg_ref, wu_ref, wd_ref, out_ref = refs[:6]
    x_ref, accg_ref, accu_ref, hidden_ref, w_ref, d_ref, sem, dsem = refs[6:]
    width = out_ref.shape[1]
    spans = [(j, min(BACK_COLUMNS, width - j)) for j in range(0, width, BACK_COLUMNS)]
    out_tiles = [wd_ref.at[0, :, pl.ds(q * width + j, w)] for j, w in spans for q in range(FOLD)]
    tiles = Stream(
        (w_ref, sem, in_tiles(wg_ref, wu_ref, start, x_ref.shape[1] // STEP)),
        (d_ref, dsem, out_tiles),
    )
    node, local = lax.axis_index("node"), lax.axis_index("local")
    size = x_ref.shape[0] * FOLD
    group, inner = unpack_row(lax.broadcasted_iota(jnp.int32, (size, size), 1), 2 * n_local)
    device = ((group & 1) ^ node) * n_local + ((group >> 1) ^ local)
    target = device * (FOLD * CAP) + inner
    back = (lax.broadcasted_iota(jnp.int32, (size, size), 0) == target).astype(jnp.bfloat16)
    unfold(blocks, x_ref)
    project(x_ref, tiles, (accg_ref, accu_ref), (ing_ref, inu_ref))
    gate_val = accg_ref[...]
    hidden_ref[...] = (gate_val / (1.0 + jnp.exp(-gate_val)) * accu_ref[...]).astype(jnp.bfloat16)
    for j, w in spans:
        values = []
        for _ in range(FOLD):
            value = jnp.dot(hidden_ref[...], tiles.take(), preferred_element_type=jnp.float32)
            values.append(value.astype(jnp.bfloat16))
        out_ref[:, j : j + w] = jnp.dot(
            back, jnp.concatenate(values, axis=0), preferred_element_type=jnp.float32
        ).astype(jnp.bfloat16)


def second_part(blocks, accs, gate_weight, up_weight, down_weight, start):
    n_local = len(blocks)
    rows = 2 * n_local * CAP
    model, hidden, whole = FOLD * blocks[0].shape[1], down_weight.shape[1], down_weight.shape[2]
    return pl.pallas_call(
        functools.partial(second_kernel, n_local, start),
        out_shape=jax.ShapeDtypeStruct((rows * FOLD, whole // FOLD), jnp.bfloat16),
        in_specs=[VMEM] * (2 + n_local) + [HBM] * 3,
        out_specs=VMEM,
        scratch_shapes=[
            pltpu.VMEM((rows, model), jnp.bfloat16),
            pltpu.VMEM((rows, hidden), jnp.float32),
            pltpu.VMEM((rows, hidden), jnp.float32),
            pltpu.VMEM((rows, hidden), jnp.bfloat16),
            pltpu.VMEM((DEPTH, STEP, hidden), jnp.bfloat16),
            pltpu.VMEM((DEPTH, hidden, BACK_COLUMNS), jnp.bfloat16),
            pltpu.SemaphoreType.DMA((DEPTH,)),
            pltpu.SemaphoreType.DMA((DEPTH,)),
        ],
        compiler_params=params(),
        cost_estimate=cost(
            2 * rows * (2 * model + whole) * hidden, 2 * (2 * model + whole) * hidden
        ),
        name="second_part",
    )(*blocks, *accs, gate_weight, up_weight, down_weight)


def column(row):
    n = row.shape[1]
    eye = lax.broadcasted_iota(jnp.int32, (n, n), 0) == lax.broadcasted_iota(jnp.int32, (n, n), 1)
    return jnp.sum(jnp.where(eye, row, jnp.zeros_like(row)), axis=1, keepdims=True)


def finish_kernel(base_ref, gates_ref, *refs):
    pieces, out_ref = refs[:-1], refs[-1]
    base = column(base_ref[...])
    gate = column(gates_ref[...])
    lane = lax.broadcasted_iota(jnp.int32, (base.shape[0], pieces[0].shape[0]), 1)
    select = [(lane == base + q * CAP).astype(jnp.bfloat16) for q in range(FOLD)]
    start = 0
    for piece in pieces:
        width = piece.shape[1]
        for q in range(FOLD):
            value = jnp.dot(select[q], piece[...], preferred_element_type=jnp.float32)
            out_ref[:, start : start + width] = (gate * value).astype(jnp.bfloat16)
            start += width


def finish(base, gates, pieces):
    tok = base.shape[1]
    model = FOLD * sum(p.shape[1] for p in pieces)
    return pl.pallas_call(
        finish_kernel,
        out_shape=jax.ShapeDtypeStruct((tok, model), jnp.bfloat16),
        in_specs=[VMEM] * (2 + len(pieces)),
        out_specs=VMEM,
        compiler_params=params(8 * 1024 * 1024),
        cost_estimate=cost(2 * tok * model * 384, 5 * tok * model),
        name="finish",
    )(base, gates.reshape(1, tok), *pieces)


def swap(block, slots):
    rows, width = block.shape
    out = lax.all_to_all(
        block.reshape(slots, rows // slots, width),
        ("node", "local"),
        split_axis=0,
        concat_axis=0,
        tiled=True,
    )
    return out.reshape(rows, width)


def swap_hops(blocks, after=None):
    n_local = len(blocks)
    out = list(blocks)
    for n, hop in enumerate(HOPS):
        block = blocks[hop]
        if after is not None:
            earlier = after[HOPS[min(n + LAG, len(HOPS) - 1)]]
            block, _ = lax.optimization_barrier((block, earlier))
        out[hop] = lax.ppermute(block, "local", [(i, i ^ hop) for i in range(n_local)])
    return out


def swap_mate(value):
    return lax.ppermute(value, "node", [(0, 1), (1, 0)])


def per_device_folded(
    tokens, experts, replicas, gates, placement, gate_weight, up_weight, down_weight
):
    tok = tokens.shape[0]
    n_local = lax.axis_size("local")
    slots = 2 * n_local
    mate = swap_mate(tokens)
    pick = (experts * placement.shape[1] + replicas).reshape(1, tok)
    spot, pieces = dispatch(placement, pick, swap_mate(pick), tokens, mate, n_local)
    early = swap_hops(pieces[0])
    late = swap_hops(pieces[1], early)
    accs = first_part(early, gate_weight, up_weight, 0)
    start = FOLD * DISPATCH[0]
    results = second_part(late, accs, gate_weight, up_weight, down_weight, start)
    return finish(spot, gates, [swap(results, slots)])


def solution(mesh):
    in_specs = (
        P(("parts", "node", "local"), None),
        P(("parts", "node", "local"), None),
        P(("parts", "node", "local"), None),
        P(("parts", "node", "local"), None),
        P(),
        P(("node", "local"), None, None),
        P(("node", "local"), None, None),
        P(("node", "local"), None, None),
    )
    out_specs = P(("parts", "node", "local"), None)

    def per_device(*args):
        folded = (
            mesh.shape["node"] == 2
            and mesh.shape["local"] == 8
            and args[1].shape[1] == 1
            and args[5].shape[2] == FF
            and args[0].shape[1] == FOLD * sum(DISPATCH)
        )
        return (per_device_folded if folded else per_device_general)(*args)

    return jax.shard_map(
        per_device, mesh=mesh, in_specs=in_specs, out_specs=out_specs, check_vma=False
    )
```
